128 devices in a mesh: grp: 4 (over z), had: 32 (over x, y, core).
Axes of the slice: x: 4, y: 4, z: 4, core: 2. Of those that a mesh axis runs over, the one named last changes fastest.
Arguments:
- embeddings: bfloat16 [131072, 1024], P(('grp', 'had'))
- targets: bfloat16 [131072, 64], P(('grp', 'had'))
- sign_bits: int32 [131072], P(('grp', 'had')), may hold values 0 or 1
- samples: int32 [128, 32, 16], P(('grp', 'had')), may hold values from 0 to 1023, as said below
- counts: int32 [128, 32], P(('grp', 'had')), may hold values from 1 to 16, as said below
Outputs:
- basis_rows: float32 [65536, 1024], P(('grp', 'had'))
- coefficients: float32 [1024, 64], replicated
The draws below stay inside these ranges and needn't reach their ends.
Inputs may be any that keep to these rules, and one draw needn't show every extreme that they name: `samples`: entry c of list [o, s] is a row number within source device s of owner o's group; the first counts[o, s] entries of a list are distinct, the rest are padding. `counts`: in every draw each owner takes 16 rows from some source device, and some owner takes 16 rows from every source device.
All inputs are finite; a program needn't handle non-finite values. No bound on the sum of `sign_bits` on one device may be relied on, other than what follows from the above.
Results may differ from the reference program's by a relative error of at most 0.0003.
Values sent between devices are 32-bit elements; how exact they have to be, the bound alone decides.
No kernel may reach another device: no remote copies, remote signals or barrier semaphores. Data moves between devices by JAX's collectives and lax.ppermute only.
A program may use at most 128 MiB of HBM per device.

```python
import math
import jax
import jax.numpy as jnp
from jax import lax

D = 1024
K = 64
ROWS_DEV = 1024
CAP = 16
TOKENS = 131072
OWNERS = 128
SLOTS = 65536
N_GRP = 4
N_HAD = 32


def shared_field(key):
    return jax.random.normal(key, (TOKENS, 2 * K), jnp.float32)


def draw_embeddings(key, part):
    common = shared_field(key)
    key = jax.random.fold_in(key, 3)
    own_key, rest_key, row_key = jax.random.split(key, 3)
    rest_field = jax.random.normal(rest_key, (TOKENS, D - 2 * K), jnp.float32)
    row_factor = jax.random.normal(row_key, (TOKENS, 1), jnp.float32)
    own_noise = jax.random.normal(own_key, (TOKENS, 2 * K), jnp.float32)
    head_field = 0.9 * common + 0.44 * own_noise
    whole_field = jnp.concatenate([head_field, rest_field], axis=1) + 0.5 * row_factor
    return whole_field.astype(jnp.bfloat16)


def draw_targets(key, part):
    common = shared_field(key)
    key = jax.random.fold_in(key, 7)
    noise_field = jax.random.normal(key, (TOKENS, K), jnp.float32)
    mixed_field = 0.8 * common[:, :K] - 0.6 * common[:, K:2 * K] + 0.5 * noise_field
    return mixed_field.astype(jnp.bfloat16)


def draw_samples(key, part):
    key = jax.random.fold_in(key, 5)
    key_first, key_second = jax.random.split(key)
    first_row = jax.random.randint(key_first, (OWNERS, N_HAD, 1), 0, ROWS_DEV)
    row_stride = 2 * jax.random.randint(key_second, (OWNERS, N_HAD, 1), 0, ROWS_DEV // 2) + 1
    slot_ids = jnp.arange(CAP, dtype=jnp.int32)[None, None, :]
    picked_rows = (first_row + slot_ids * row_stride) % ROWS_DEV
    return picked_rows.astype(jnp.int32)


def draw_counts(key, part):
    key = jax.random.fold_in(key, 11)
    key_first, key_second, key_third = jax.random.split(key, 3)
    draw_values = jax.random.randint(key_first, (OWNERS, N_HAD), 1, CAP + 1)
    heavy_source = jax.random.randint(key_second, (OWNERS, 1), 0, N_HAD)
    source_ids = jnp.arange(N_HAD, dtype=jnp.int32)[None, :]
    owner_ids = jnp.arange(OWNERS, dtype=jnp.int32)[:, None]
    draw_values = jnp.where(source_ids == heavy_source, CAP, draw_values)
    full_owner = jax.random.randint(key_third, (), 0, OWNERS)
    draw_values = jnp.where(owner_ids == full_owner, CAP, draw_values)
    light_source = (heavy_source + 1) % N_HAD
    light_owner = (full_owner + 1) % OWNERS
    draw_values = jnp.where((owner_ids == light_owner) & (source_ids == light_source), 1, draw_values)
    return draw_values.astype(jnp.int32)


def plant(drawn, key, least, largest):
    longest = drawn.shape.index(max(drawn.shape))
    spots = []
    for shift in (0, 1):
        where = [jax.random.randint(jax.random.fold_in(key, axis), (), 0, length) for axis, length in enumerate(drawn.shape)]
        where[longest] = (where[longest] + shift) % drawn.shape[longest]
        spots.append(tuple(where))
    return drawn.at[spots[0]].set(least).at[spots[1]].set(largest)


def setup_inputs(seed: int = 0) -> dict:
    splits = jax.random.split(jax.random.key(seed), 6)
    return {
        "embeddings": draw_embeddings(jax.random.fold_in(splits[5], 71), 0),
        "targets": draw_targets(jax.random.fold_in(splits[5], 71), 0),
        "sign_bits": plant((jax.random.randint(splits[2], (TOKENS,), 0, 2) < 1).astype(jnp.int32), jax.random.fold_in(splits[2], 1), 0, 1),
        "samples": draw_samples(jax.random.fold_in(splits[5], 71), 0),
        "counts": draw_counts(jax.random.fold_in(splits[5], 71), 0),
    }


def hadamard_table(size):
    row_ids = jnp.arange(size, dtype=jnp.int32)[:, None]
    col_ids = jnp.arange(size, dtype=jnp.int32)[None, :]
    correlation = jnp.bitwise_and(row_ids, col_ids)
    parity = jnp.zeros((size, size), jnp.int32)
    for bit_pos in range(max(size.bit_length(), 1)):
        parity = jnp.bitwise_xor(parity, jnp.bitwise_and(jnp.right_shift(correlation, bit_pos), 1))
    return (1 - 2 * parity).astype(jnp.float32)

def reference(embeddings, targets, sign_bits, samples, counts):
    columns = D + K
    factor = (1 - 2 * sign_bits).astype(jnp.bfloat16)[:, None]
    joined = jnp.concatenate([embeddings, targets], axis=1) * factor
    joined = joined.reshape(N_GRP, N_HAD, ROWS_DEV, columns)
    inner_table = hadamard_table(ROWS_DEV)
    outer_table = hadamard_table(N_HAD)
    norm_factor = 1.0 / math.sqrt(ROWS_DEV * N_HAD)
    owner_lists = samples.reshape(N_GRP, N_HAD, N_HAD, CAP)
    owner_counts = counts.reshape(N_GRP, N_HAD, N_HAD)

    def one_group(group_args):
        pieces, lists, live_counts = group_args
        inner_mix = jnp.einsum('rq,hqc->hrc', inner_table, pieces.astype(jnp.float32), precision=lax.Precision.HIGHEST)
        mixed_rows = jnp.einsum('ab,brc->arc', outer_table, inner_mix, precision=lax.Precision.HIGHEST) * norm_factor
        source_ids = jnp.arange(N_HAD, dtype=jnp.int32)[None, :, None]
        picked = mixed_rows[source_ids, lists]
        live_slots = jnp.arange(CAP, dtype=jnp.int32)[None, None, :] < live_counts[:, :, None]
        picked = jnp.where(live_slots[..., None], picked, jnp.zeros_like(picked))
        flat_rows = picked.reshape(-1, columns)
        gram_part = jnp.dot(flat_rows.T, flat_rows[:, :D], precision=lax.Precision.HIGHEST)
        return (picked, gram_part)
    sketch, gram_parts = lax.map(one_group, (joined, owner_lists, owner_counts))
    gram_total = lax.optimization_barrier(jnp.sum(gram_parts, axis=0)) * (1.0 / SLOTS)
    system = gram_total[:D] + 0.05 * jnp.eye(D, dtype=jnp.float32)
    factor_lower = jnp.linalg.cholesky(system)
    sketch_rows = sketch.reshape(-1, columns)[:, :D]
    basis_rows = lax.linalg.triangular_solve(factor_lower, sketch_rows, left_side=False, lower=True, transpose_a=True)
    right_side = gram_total[D:].T
    middle = lax.linalg.triangular_solve(factor_lower, right_side, left_side=True, lower=True)
    coefficients = lax.linalg.triangular_solve(factor_lower, middle, left_side=True, lower=True, transpose_a=True)
    return (basis_rows, coefficients)
```

```python
import math

import jax
import jax.numpy as jnp
from jax import lax
from jax.experimental import pallas as pl
from jax.experimental.pallas import tpu as pltpu
from jax.sharding import PartitionSpec as P

D = 1024
K = 64
CAP = 16
HAD = 32
ROWS = 1024
SLOTS = 512
LANES = 128
BLOCK = 128
BLOCKS = D // BLOCK
RIDGE = 0.05
BOTH = ("grp", "had")

PIECE = 280
LIST_ROW = 272
BACK = 136
HIGHEST = lax.Precision.HIGHEST
COLUMN_ROWS = [D + K - BLOCK * j for j in range(BLOCKS)]
COLUMN_START = [sum(COLUMN_ROWS[:j]) for j in range(BLOCKS)]
PACKED = sum(COLUMN_ROWS)
MIB = 1024 * 1024


def call(kernel, out_shape, scratch, vmem_mib, *args):
    return pl.pallas_call(
        kernel,
        out_shape=out_shape,
        in_specs=[pl.BlockSpec(memory_space=pltpu.VMEM)] * len(args),
        out_specs=jax.tree.map(lambda _: pl.BlockSpec(memory_space=pltpu.VMEM), out_shape),
        scratch_shapes=scratch,
        compiler_params=pltpu.CompilerParams(vmem_limit_bytes=vmem_mib * MIB),
    )(*args)


def f32(*shape):
    return jax.ShapeDtypeStruct(shape, jnp.float32)


def spread_kernel(embeddings, targets, factor, lists, out):
    for tile in range(8):
        rows = slice(tile * LANES, (tile + 1) * LANES)
        sign = factor[tile : tile + 1, :]
        columns = embeddings[rows, :].astype(jnp.float32).T * sign
        out[:, tile * 32 : (tile + 1) * 32, :] = columns.reshape(HAD, 32, LANES)
        extra = targets[rows, :].astype(jnp.float32).T * sign
        for device in range(HAD):
            for half in range(2):
                row = 256 + 2 * tile + half
                source = 32 * half + device
                out[device, row : row + 1, :] = extra[source : source + 1, :]
    tail = jnp.concatenate([lists[...], jnp.zeros((4, LANES), jnp.float32)], axis=0)
    out[:, LIST_ROW:PIECE, :] = jnp.broadcast_to(tail[None], (HAD, 8, LANES))


def swap_segments(values):
    values = list(values)
    lane = lax.broadcasted_iota(jnp.int32, values[0].shape, values[0].ndim - 1)
    for bit in range(3):
        step = 1 << bit
        upper = jnp.bitwise_and(jnp.right_shift(lane, 4 + bit), 1) == 1
        for low in range(8):
            if low & step:
                continue
            first, second = values[low], values[low + step]
            values[low] = jnp.where(upper, pltpu.roll(second, 16 * step, 1), first)
            values[low + step] = jnp.where(upper, second, pltpu.roll(first, LANES - 16 * step, 1))
    return values


def signs(row_bits, count):
    both = jnp.bitwise_and(lax.broadcasted_iota(jnp.int32, (count, row_bits.shape[1]), 0), row_bits)
    for shift in (4, 2, 1):
        both = jnp.bitwise_xor(both, jnp.right_shift(both, shift))
    return (1 - 2 * jnp.bitwise_and(both, 1)).astype(jnp.float32)


def mix_kernel(pieces, out, mixed, lists, table, picked, extra):
    scale = 1.0 / math.sqrt(ROWS * HAD)

    def butterfly(chunk, _):
        rows = pl.ds(pl.multiple_of(chunk * 8, 8), 8)
        values = [pieces[device, rows, :] for device in range(HAD)]
        for bit in range(5):
            step = 1 << bit
            for low in range(HAD):
                if low & step:
                    continue
                first, second = values[low], values[low + step]
                values[low], values[low + step] = first + second, first - second
        for source in range(HAD):
            mixed[source, rows, :] = values[source]
        return 0

    lax.fori_loop(0, LIST_ROW // 8, butterfly, 0)
    for high in range(4):
        received = [pieces[high * 8 + low, LIST_ROW:PIECE, :] for low in range(8)]
        for low, value in enumerate(swap_segments(received)):
            lists[low, :, high * LANES : (high + 1) * LANES] = value

    def source_group(group, _):
        for low in range(8):
            source = group * 8 + low
            rows = lists[low, pl.ds(group, 1), :].astype(jnp.int32)
            fine = signs(jnp.bitwise_and(rows, 31), 32).astype(jnp.bfloat16)
            coarse = signs(jnp.right_shift(rows, 5), 32).astype(jnp.bfloat16)
            for step in range(32):
                table[low % 2, step * 32 : (step + 1) * 32, :] = fine * coarse[step : step + 1, :]
            main = jnp.concatenate([mixed[source, t * 32 : (t + 1) * 32, :] for t in range(8)], axis=1)
            tail = mixed[source, 256:272, :]
            tail = jnp.concatenate([tail[2 * t : 2 * t + 2, :] for t in range(8)], axis=1)
            main_high = main.astype(jnp.bfloat16).astype(jnp.float32)
            tail_high = tail.astype(jnp.bfloat16).astype(jnp.float32)
            left = jnp.concatenate(
                [
                    main_high,
                    main - main_high,
                    tail_high,
                    tail - tail_high,
                    jnp.zeros((4, ROWS), jnp.float32),
                ],
                axis=0,
            ).astype(jnp.bfloat16)
            product = jnp.dot(left, table[low % 2], preferred_element_type=jnp.float32)
            picked[low, 0:32, :] = (product[0:32] + product[32:64]) * scale
            picked[low, 32:34, :] = (product[64:66] + product[66:68]) * scale
        for high in range(4):
            lanes = slice(high * LANES, (high + 1) * LANES)
            moved = swap_segments([picked[low, :, lanes] for low in range(8)])
            for low, value in enumerate(moved):
                out[high * 8 + low, pl.ds(pl.multiple_of(group * 32, 32), 32), :] = value[0:32]
                extra[group, high * 8 + low] = value[32:40]
        return 0

    lax.fori_loop(0, 4, source_group, 0)
    for group in range(4):
        for owner in range(HAD):
            out[owner, 128 + 2 * group : 130 + 2 * group, :] = extra[group, owner, 0:2, :]


def gram_kernel(received, live, gram, sketch, flipped):
    for group in range(4):
        lanes = slice(group * LANES, (group + 1) * LANES)
        keep = live[group : group + 1, :] > 0
        part = received[:, group * 32 : (group + 1) * 32, :].reshape(D, LANES)
        part = jnp.where(keep, part, 0.0)
        flipped[0:D, lanes] = part
        sketch[lanes, :] = part.T
        for half in range(2):
            for device in range(HAD):
                row = D + 32 * half + device
                source = 128 + 2 * group + half
                value = received[device, source : source + 1, :]
                flipped[row : row + 1, lanes] = jnp.where(keep, value, 0.0)
    for pair in range(BLOCKS // 2):
        first = 256 * pair
        block = jnp.dot(
            flipped[first:, :],
            sketch[:, first : first + 256],
            precision=HIGHEST,
            preferred_element_type=jnp.float32,
        )
        left, right = 2 * pair, 2 * pair + 1
        gram[COLUMN_START[left] : COLUMN_START[left] + COLUMN_ROWS[left], :] = block[:, :BLOCK]
        gram[COLUMN_START[right] : COLUMN_START[right] + COLUMN_ROWS[right], :] = block[BLOCK:, BLOCK:]


def across_lanes(value, lane):
    return jnp.broadcast_to(value[:, lane : lane + 1], value.shape)


def down_rows(value, row):
    return jnp.broadcast_to(value[row : row + 1, :], value.shape)


def inverse_factor(block):
    rows = [block[8 * g : 8 * g + 8, :] for g in range(16)]
    sub = lax.broadcasted_iota(jnp.int32, (8, LANES), 0)
    lane = lax.broadcasted_iota(jnp.int32, (8, LANES), 1)
    result = []
    for g in range(16):
        own = jnp.right_shift(lane, 3) == g
        columns = [across_lanes(rows[g], 8 * g + k) for k in range(8)]
        value = jnp.where(own, jnp.where(lane == 8 * g + sub, 1.0, 0.0), rows[g])
        finished = jnp.zeros((8, LANES), jnp.float32)
        for i in range(8):
            pivot = down_rows(columns[i], i)
            inverse = 1.0 / pivot
            root = lax.rsqrt(pivot)
            root = root * (1.5 - 0.5 * pivot * root * root)
            here = sub == i
            row = down_rows(value, i)
            finished = jnp.where(here, row * root, finished)
            weight = columns[i] * inverse
            value = jnp.where(here, row * inverse, value - weight * row)
            for k in range(i + 1, 8):
                entry = down_rows(columns[k], i)
                columns[k] = jnp.where(here, entry * inverse, columns[k] - weight * entry)
        result.append(jnp.where(lane <= 8 * g + sub, finished, 0.0))
        solved = [down_rows(value, k) for k in range(8)]
        for h in range(g + 1, 16):
            terms = [across_lanes(rows[h], 8 * g + k) * solved[k] for k in range(8)]
            while len(terms) > 1:
                terms = [terms[t] + terms[t + 1] for t in range(0, len(terms), 2)]
            rows[h] = jnp.where(own, 0.0, rows[h]) - terms[0]
    return jnp.concatenate(result, axis=0)


def times_transposed(left, right):
    return lax.dot_general(
        left,
        right,
        (((1,), (1,)), ((), ())),
        precision=HIGHEST,
        preferred_element_type=jnp.float32,
    )


def times(left, right):
    return jnp.dot(left, right, precision=HIGHEST, preferred_element_type=jnp.float32)


def solve_kernel(slot_total, gram, sketch, basis, coefficients, lower, inverses):
    row = lax.broadcasted_iota(jnp.int32, (BLOCK, BLOCK), 0)
    column = lax.broadcasted_iota(jnp.int32, (BLOCK, BLOCK), 1)
    ridge = jnp.where(row == column, RIDGE, 0.0)
    for j in range(BLOCKS):
        start = COLUMN_START[j]
        lower[start : start + BLOCK, :] = gram[start : start + BLOCK, :] * (1.0 / slot_total) + ridge
        rest = slice(start + BLOCK, start + COLUMN_ROWS[j])
        lower[rest, :] = gram[rest, :] * (1.0 / slot_total)
    basis[...] = sketch[...]
    for j in range(BLOCKS):
        start = COLUMN_START[j]
        own = slice(BLOCK * j, BLOCK * (j + 1))
        inverse = inverse_factor(lower[start : start + BLOCK, :])
        inverses[j] = inverse
        below = times_transposed(lower[start + BLOCK : start + COLUMN_ROWS[j], :], inverse)
        lower[start + BLOCK : start + COLUMN_ROWS[j], :] = below
        for i in range(j + 1, BLOCKS):
            first = BLOCK * (i - j - 1)
            target = slice(COLUMN_START[i], COLUMN_START[i] + COLUMN_ROWS[i])
            lower[target, :] -= times_transposed(below[first:], below[first : first + BLOCK])
        solved = times_transposed(basis[:, own], inverse)
        basis[:, own] = solved
        if j < BLOCKS - 1:
            rest = slice(BLOCK * (j + 1), D)
            basis[:, rest] -= times_transposed(solved, below[: BLOCK * (BLOCKS - 1 - j)])
    middle = []
    for j in range(BLOCKS):
        end = COLUMN_START[j] + COLUMN_ROWS[j]
        middle.append(lower[end - K : end, :])
    for j in reversed(range(BLOCKS)):
        value = times(middle[j], inverses[j])
        coefficients[BLOCK * j : BLOCK * (j + 1), :] = value.T
        for i in range(j):
            start = COLUMN_START[i] + BLOCK * (j - i)
            middle[i] = middle[i] - times(value, lower[start : start + BLOCK, :])


def total(gram):
    return lax.psum(gram, BOTH)


def on_device(embeddings, targets, sign_bits, samples, counts):
    had_size = lax.axis_size("had")
    factor = (1 - 2 * sign_bits).astype(jnp.float32).reshape(8, LANES)
    lists = samples.reshape(4, LANES).astype(jnp.float32)
    pieces = call(spread_kernel, f32(HAD, PIECE, LANES), [], 40, embeddings, targets, factor, lists)
    pieces = lax.all_to_all(pieces, "had", split_axis=0, concat_axis=0, tiled=True)
    outgoing = call(
        mix_kernel,
        f32(HAD, BACK, LANES),
        [
            pltpu.VMEM((HAD, LIST_ROW, LANES), jnp.float32),
            pltpu.VMEM((8, 8, SLOTS), jnp.float32),
            pltpu.VMEM((2, ROWS, SLOTS), jnp.bfloat16),
            pltpu.VMEM((8, 40, SLOTS), jnp.float32),
            pltpu.VMEM((4, HAD, 8, LANES), jnp.float32),
        ],
        40,
        pieces,
    )
    received = lax.all_to_all(outgoing, "had", split_axis=0, concat_axis=0, tiled=True)
    slot = jnp.arange(CAP, dtype=jnp.int32)[None, :]
    live = (slot < counts.reshape(had_size)[:, None]).astype(jnp.float32).reshape(4, LANES)
    gram, sketch = call(
        gram_kernel,
        (f32(PACKED, LANES), f32(SLOTS, D)),
        [pltpu.VMEM((D + K, SLOTS), jnp.float32)],
        40,
        received,
        live,
    )
    gram = total(gram)
    slot_total = lax.axis_size("grp") * had_size * SLOTS
    return call(
        lambda *refs: solve_kernel(slot_total, *refs),
        (f32(SLOTS, D), f32(D, K)),
        [
            pltpu.VMEM((PACKED, LANES), jnp.float32),
            pltpu.VMEM((BLOCKS, BLOCK, BLOCK), jnp.float32),
        ],
        40,
        gram,
        sketch,
    )


def solution(mesh):
    placed = (
        P(("grp", "had"), None),
        P(("grp", "had"), None),
        P(("grp", "had")),
        P(("grp", "had"), None, None),
        P(("grp", "had"), None),
    )
    return jax.shard_map(
        on_device,
        mesh=mesh,
        in_specs=placed,
        out_specs=(P(("grp", "had"), None), P()),
        check_vma=False,
    )
```

```python
import math

import jax
import jax.numpy as jnp
from jax import lax
from jax.experimental import pallas as pl
from jax.experimental.pallas import tpu as pltpu
from jax.sharding import PartitionSpec as P

D = 1024
K = 64
CAP = 16
HAD = 32
ROWS = 1024
SLOTS = 512
LANES = 128
BLOCK = 128
BLOCKS = D // BLOCK
RIDGE = 0.05
BOTH = ("grp", "had")

PIECE = 280
LIST_ROW = 272
BACK = 136
HIGHEST = lax.Precision.HIGHEST
COLUMN_ROWS = [D + K - BLOCK * j for j in range(BLOCKS)]
COLUMN_START = [sum(COLUMN_ROWS[:j]) for j in range(BLOCKS)]
PACKED = sum(COLUMN_ROWS)
MIB = 1024 * 1024


def call(kernel, out_shape, scratch, vmem_mib, *args):
    return pl.pallas_call(
        kernel,
        out_shape=out_shape,
        in_specs=[pl.BlockSpec(memory_space=pltpu.VMEM)] * len(args),
        out_specs=jax.tree.map(lambda _: pl.BlockSpec(memory_space=pltpu.VMEM), out_shape),
        scratch_shapes=scratch,
        compiler_params=pltpu.CompilerParams(vmem_limit_bytes=vmem_mib * MIB),
    )(*args)


def f32(*shape):
    return jax.ShapeDtypeStruct(shape, jnp.float32)


def spread_kernel(embeddings, targets, factor, lists, out):
    for tile in range(8):
        rows = slice(tile * LANES, (tile + 1) * LANES)
        sign = factor[tile : tile + 1, :]
        columns = embeddings[rows, :].astype(jnp.float32).T * sign
        out[:, tile * 32 : (tile + 1) * 32, :] = columns.reshape(HAD, 32, LANES)
        extra = targets[rows, :].astype(jnp.float32).T * sign
        for device in range(HAD):
            for half in range(2):
                row = 256 + 2 * tile + half
                source = 32 * half + device
                out[device, row : row + 1, :] = extra[source : source + 1, :]
    tail = jnp.concatenate([lists[...], jnp.zeros((4, LANES), jnp.float32)], axis=0)
    out[:, LIST_ROW:PIECE, :] = jnp.broadcast_to(tail[None], (HAD, 8, LANES))


def swap_segments(values):
    values = list(values)
    lane = lax.broadcasted_iota(jnp.int32, values[0].shape, values[0].ndim - 1)
    for bit in range(3):
        step = 1 << bit
        upper = jnp.bitwise_and(jnp.right_shift(lane, 4 + bit), 1) == 1
        for low in range(8):
            if low & step:
                continue
            first, second = values[low], values[low + step]
            values[low] = jnp.where(upper, pltpu.roll(second, 16 * step, 1), first)
            values[low + step] = jnp.where(upper, second, pltpu.roll(first, LANES - 16 * step, 1))
    return values


def signs(row_bits, count):
    both = jnp.bitwise_and(lax.broadcasted_iota(jnp.int32, (count, row_bits.shape[1]), 0), row_bits)
    for shift in (4, 2, 1):
        both = jnp.bitwise_xor(both, jnp.right_shift(both, shift))
    return (1 - 2 * jnp.bitwise_and(both, 1)).astype(jnp.float32)


def mix_kernel(pieces, out, mixed, lists, table, picked, extra):
    scale = 1.0 / math.sqrt(ROWS * HAD)

    def butterfly(chunk, _):
        rows = pl.ds(pl.multiple_of(chunk * 8, 8), 8)
        values = [pieces[device, rows, :] for device in range(HAD)]
        for bit in range(5):
            step = 1 << bit
            for low in range(HAD):
                if low & step:
                    continue
                first, second = values[low], values[low + step]
                values[low], values[low + step] = first + second, first - second
        for source in range(HAD):
            mixed[source, rows, :] = values[source]
        return 0

    lax.fori_loop(0, LIST_ROW // 8, butterfly, 0)
    for high in range(4):
        received = [pieces[high * 8 + low, LIST_ROW:PIECE, :] for low in range(8)]
        for low, value in enumerate(swap_segments(received)):
            lists[low, :, high * LANES : (high + 1) * LANES] = value

    def source_group(group, _):
        for low in range(8):
            source = group * 8 + low
            rows = lists[low, pl.ds(group, 1), :].astype(jnp.int32)
            fine = signs(jnp.bitwise_and(rows, 31), 32).astype(jnp.bfloat16)
            coarse = signs(jnp.right_shift(rows, 5), 32).astype(jnp.bfloat16)
            for step in range(32):
                table[low % 2, step * 32 : (step + 1) * 32, :] = fine * coarse[step : step + 1, :]
            main = jnp.concatenate([mixed[source, t * 32 : (t + 1) * 32, :] for t in range(8)], axis=1)
            tail = mixed[source, 256:272, :]
            tail = jnp.concatenate([tail[2 * t : 2 * t + 2, :] for t in range(8)], axis=1)
            main_high = main.astype(jnp.bfloat16).astype(jnp.float32)
            tail_high = tail.astype(jnp.bfloat16).astype(jnp.float32)
            left = jnp.concatenate(
                [
                    main_high,
                    main - main_high,
                    tail_high,
                    tail - tail_high,
                    jnp.zeros((4, ROWS), jnp.float32),
                ],
                axis=0,
            ).astype(jnp.bfloat16)
            product = jnp.dot(left, table[low % 2], preferred_element_type=jnp.float32)
            picked[low, 0:32, :] = (product[0:32] + product[32:64]) * scale
            picked[low, 32:34, :] = (product[64:66] + product[66:68]) * scale
        for high in range(4):
            lanes = slice(high * LANES, (high + 1) * LANES)
            moved = swap_segments([picked[low, :, lanes] for low in range(8)])
            for low, value in enumerate(moved):
                out[high * 8 + low, pl.ds(pl.multiple_of(group * 32, 32), 32), :] = value[0:32]
                extra[group, high * 8 + low] = value[32:40]
        return 0

    lax.fori_loop(0, 4, source_group, 0)
    for group in range(4):
        for owner in range(HAD):
            out[owner, 128 + 2 * group : 130 + 2 * group, :] = extra[group, owner, 0:2, :]


def gram_kernel(received, live, gram, sketch, flipped):
    for group in range(4):
        lanes = slice(group * LANES, (group + 1) * LANES)
        keep = live[group : group + 1, :] > 0
        part = received[:, group * 32 : (group + 1) * 32, :].reshape(D, LANES)
        part = jnp.where(keep, part, 0.0)
        flipped[0:D, lanes] = part
        sketch[lanes, :] = part.T
        for half in range(2):
            for device in range(HAD):
                row = D + 32 * half + device
                source = 128 + 2 * group + half
                value = received[device, source : source + 1, :]
                flipped[row : row + 1, lanes] = jnp.where(keep, value, 0.0)
    for pair in range(BLOCKS // 2):
        first = 256 * pair
        block = jnp.dot(
            flipped[first:, :],
            sketch[:, first : first + 256],
            precision=HIGHEST,
            preferred_element_type=jnp.float32,
        )
        left, right = 2 * pair, 2 * pair + 1
        gram[COLUMN_START[left] : COLUMN_START[left] + COLUMN_ROWS[left], :] = block[:, :BLOCK]
        gram[COLUMN_START[right] : COLUMN_START[right] + COLUMN_ROWS[right], :] = block[BLOCK:, BLOCK:]


def across_lanes(value, lane):
    return jnp.broadcast_to(value[:, lane : lane + 1], value.shape)


def down_rows(value, row):
    return jnp.broadcast_to(value[row : row + 1, :], value.shape)


def inverse_factor(block):
    rows = [block[8 * g : 8 * g + 8, :] for g in range(16)]
    sub = lax.broadcasted_iota(jnp.int32, (8, LANES), 0)
    lane = lax.broadcasted_iota(jnp.int32, (8, LANES), 1)
    result = []
    for g in range(16):
        own = jnp.right_shift(lane, 3) == g
        columns = [across_lanes(rows[g], 8 * g + k) for k in range(8)]
        value = jnp.where(own, jnp.where(lane == 8 * g + sub, 1.0, 0.0), rows[g])
        finished = jnp.zeros((8, LANES), jnp.float32)
        for i in range(8):
            pivot = down_rows(columns[i], i)
            inverse = 1.0 / pivot
            root = lax.rsqrt(pivot)
            root = root * (1.5 - 0.5 * pivot * root * root)
            here = sub == i
            row = down_rows(value, i)
            finished = jnp.where(here, row * root, finished)
            weight = columns[i] * inverse
            value = jnp.where(here, row * inverse, value - weight * row)
            for k in range(i + 1, 8):
                entry = down_rows(columns[k], i)
                columns[k] = jnp.where(here, entry * inverse, columns[k] - weight * entry)
        result.append(jnp.where(lane <= 8 * g + sub, finished, 0.0))
        solved = [down_rows(value, k) for k in range(8)]
        for h in range(g + 1, 16):
            terms = [across_lanes(rows[h], 8 * g + k) * solved[k] for k in range(8)]
            while len(terms) > 1:
                terms = [terms[t] + terms[t + 1] for t in range(0, len(terms), 2)]
            rows[h] = jnp.where(own, 0.0, rows[h]) - terms[0]
    return jnp.concatenate(result, axis=0)


def times_transposed(left, right):
    return lax.dot_general(
        left,
        right,
        (((1,), (1,)), ((), ())),
        precision=HIGHEST,
        preferred_element_type=jnp.float32,
    )


def times(left, right):
    return jnp.dot(left, right, precision=HIGHEST, preferred_element_type=jnp.float32)


def solve_kernel(slot_total, gram, sketch, basis, coefficients, lower, inverses):
    row = lax.broadcasted_iota(jnp.int32, (BLOCK, BLOCK), 0)
    column = lax.broadcasted_iota(jnp.int32, (BLOCK, BLOCK), 1)
    ridge = jnp.where(row == column, RIDGE, 0.0)
    for j in range(BLOCKS):
        start = COLUMN_START[j]
        lower[start : start + BLOCK, :] = gram[start : start + BLOCK, :] * (1.0 / slot_total) + ridge
        rest = slice(start + BLOCK, start + COLUMN_ROWS[j])
        lower[rest, :] = gram[rest, :] * (1.0 / slot_total)
    basis[...] = sketch[...]
    for j in range(BLOCKS):
        start = COLUMN_START[j]
        own = slice(BLOCK * j, BLOCK * (j + 1))
        inverse = inverse_factor(lower[start : start + BLOCK, :])
        inverses[j] = inverse
        below = times_transposed(lower[start + BLOCK : start + COLUMN_ROWS[j], :], inverse)
        lower[start + BLOCK : start + COLUMN_ROWS[j], :] = below
        for i in range(j + 1, BLOCKS):
            first = BLOCK * (i - j - 1)
            target = slice(COLUMN_START[i], COLUMN_START[i] + COLUMN_ROWS[i])
            lower[target, :] -= times_transposed(below[first:], below[first : first + BLOCK])
        solved = times_transposed(basis[:, own], inverse)
        basis[:, own] = solved
        if j < BLOCKS - 1:
            rest = slice(BLOCK * (j + 1), D)
            basis[:, rest] -= times_transposed(solved, below[: BLOCK * (BLOCKS - 1 - j)])
    middle = []
    for j in range(BLOCKS):
        end = COLUMN_START[j] + COLUMN_ROWS[j]
        middle.append(lower[end - K : end, :])
    for j in reversed(range(BLOCKS)):
        value = times(middle[j], inverses[j])
        coefficients[BLOCK * j : BLOCK * (j + 1), :] = value.T
        for i in range(j):
            start = COLUMN_START[i] + BLOCK * (j - i)
            middle[i] = middle[i] - times(value, lower[start : start + BLOCK, :])


def swap_cores(value):
    return lax.ppermute(value, "had", [(device, device ^ 1) for device in range(HAD)])


def shift_groups(value, step):
    size = lax.axis_size("grp")
    return lax.ppermute(value, "grp", [(group, (group + step) % size) for group in range(size)])


def total(gram):
    core = jnp.bitwise_and(lax.axis_index("had"), 1)
    half = PACKED // 2
    mine = lax.dynamic_slice_in_dim(gram, core * half, half, 0)
    other = lax.dynamic_slice_in_dim(gram, (1 - core) * half, half, 0)
    part = mine + swap_cores(other)
    chips = [[2 * chip + own for chip in range(HAD // 2)] for own in range(2)]
    part = part.reshape(HAD // 2, half // (HAD // 2), LANES)
    part = lax.all_to_all(part, "had", 0, 0, tiled=True, axis_index_groups=chips)
    part = jnp.sum(part, axis=0)
    part = part + shift_groups(part, 2)
    part = part + shift_groups(part, 1)
    part = jnp.broadcast_to(part[None], (HAD // 2, *part.shape))
    part = lax.all_to_all(part, "had", 0, 0, tiled=True, axis_index_groups=chips)
    part = part.reshape(half, LANES)
    other = swap_cores(part)
    first = jnp.where(core == 0, part, other)
    second = jnp.where(core == 0, other, part)
    return jnp.concatenate([first, second], axis=0)


def on_device(embeddings, targets, sign_bits, samples, counts):
    had_size = lax.axis_size("had")
    factor = (1 - 2 * sign_bits).astype(jnp.float32).reshape(8, LANES)
    lists = samples.reshape(4, LANES).astype(jnp.float32)
    pieces = call(spread_kernel, f32(HAD, PIECE, LANES), [], 40, embeddings, targets, factor, lists)
    pieces = lax.all_to_all(pieces, "had", split_axis=0, concat_axis=0, tiled=True)
    outgoing = call(
        mix_kernel,
        f32(HAD, BACK, LANES),
        [
            pltpu.VMEM((HAD, LIST_ROW, LANES), jnp.float32),
            pltpu.VMEM((8, 8, SLOTS), jnp.float32),
            pltpu.VMEM((2, ROWS, SLOTS), jnp.bfloat16),
            pltpu.VMEM((8, 40, SLOTS), jnp.float32),
            pltpu.VMEM((4, HAD, 8, LANES), jnp.float32),
        ],
        40,
        pieces,
    )
    received = lax.all_to_all(outgoing, "had", split_axis=0, concat_axis=0, tiled=True)
    slot = jnp.arange(CAP, dtype=jnp.int32)[None, :]
    live = (slot < counts.reshape(had_size)[:, None]).astype(jnp.float32).reshape(4, LANES)
    gram, sketch = call(
        gram_kernel,
        (f32(PACKED, LANES), f32(SLOTS, D)),
        [pltpu.VMEM((D + K, SLOTS), jnp.float32)],
        40,
        received,
        live,
    )
    gram = total(gram)
    slot_total = lax.axis_size("grp") * had_size * SLOTS
    return call(
        lambda *refs: solve_kernel(slot_total, *refs),
        (f32(SLOTS, D), f32(D, K)),
        [
            pltpu.VMEM((PACKED, LANES), jnp.float32),
            pltpu.VMEM((BLOCKS, BLOCK, BLOCK), jnp.float32),
        ],
        40,
        gram,
        sketch,
    )


def solution(mesh):
    placed = (
        P(("grp", "had"), None),
        P(("grp", "had"), None),
        P(("grp", "had")),
        P(("grp", "had"), None, None),
        P(("grp", "had"), None),
    )
    return jax.shard_map(
        on_device,
        mesh=mesh,
        in_specs=placed,
        out_specs=(P(("grp", "had"), None), P()),
        check_vma=False,
    )
```

```python
import math

import jax
import jax.numpy as jnp
from jax import lax
from jax.experimental import pallas as pl
from jax.experimental.pallas import tpu as pltpu
from jax.sharding import PartitionSpec as P

D = 1024
K = 64
CAP = 16
HAD = 32
ROWS = 1024
SLOTS = 512
LANES = 128
BLOCK = 128
BLOCKS = D // BLOCK
RIDGE = 0.05
BOTH = ("grp", "had")

PIECE = 280
LIST_ROW = 272
BACK = 136
HIGHEST = lax.Precision.HIGHEST
COLUMN_ROWS = [D + K - BLOCK * j for j in range(BLOCKS)]
COLUMN_START = [sum(COLUMN_ROWS[:j]) for j in range(BLOCKS)]
PACKED = sum(COLUMN_ROWS)
MIB = 1024 * 1024
NEAR_ROWS = 2
RUN_ENDS = {8: 0, 12: 8, 16: 12}


def call(kernel, out_shape, scratch, vmem_mib, *args):
    return pl.pallas_call(
        kernel,
        out_shape=out_shape,
        in_specs=[pl.BlockSpec(memory_space=pltpu.VMEM)] * len(args),
        out_specs=jax.tree.map(lambda _: pl.BlockSpec(memory_space=pltpu.VMEM), out_shape),
        scratch_shapes=scratch,
        compiler_params=pltpu.CompilerParams(vmem_limit_bytes=vmem_mib * MIB),
    )(*args)


def f32(*shape):
    return jax.ShapeDtypeStruct(shape, jnp.float32)


def spread_kernel(embeddings, targets, factor, lists, out):
    for tile in range(8):
        rows = slice(tile * LANES, (tile + 1) * LANES)
        sign = factor[tile : tile + 1, :]
        columns = embeddings[rows, :].astype(jnp.float32).T * sign
        out[:, tile * 32 : (tile + 1) * 32, :] = columns.reshape(HAD, 32, LANES)
        extra = targets[rows, :].astype(jnp.float32).T * sign
        for device in range(HAD):
            for half in range(2):
                row = 256 + 2 * tile + half
                source = 32 * half + device
                out[device, row : row + 1, :] = extra[source : source + 1, :]
    tail = jnp.concatenate([lists[...], jnp.zeros((4, LANES), jnp.float32)], axis=0)
    out[:, LIST_ROW:PIECE, :] = jnp.broadcast_to(tail[None], (HAD, 8, LANES))


def swap_segments(values):
    values = list(values)
    lane = lax.broadcasted_iota(jnp.int32, values[0].shape, values[0].ndim - 1)
    for bit in range(3):
        step = 1 << bit
        upper = jnp.bitwise_and(jnp.right_shift(lane, 4 + bit), 1) == 1
        for low in range(8):
            if low & step:
                continue
            first, second = values[low], values[low + step]
            values[low] = jnp.where(upper, pltpu.roll(second, 16 * step, 1), first)
            values[low + step] = jnp.where(upper, second, pltpu.roll(first, LANES - 16 * step, 1))
    return values


def signs(row_bits, count):
    both = jnp.bitwise_and(lax.broadcasted_iota(jnp.int32, (count, row_bits.shape[1]), 0), row_bits)
    for shift in (4, 2, 1):
        both = jnp.bitwise_xor(both, jnp.right_shift(both, shift))
    return (1 - 2 * jnp.bitwise_and(both, 1)).astype(jnp.float32)


def mix_kernel(pieces, out, mixed, lists, table, picked, extra):
    scale = 1.0 / math.sqrt(ROWS * HAD)

    def butterfly(chunk, _):
        rows = pl.ds(pl.multiple_of(chunk * 8, 8), 8)
        values = [pieces[device, rows, :] for device in range(HAD)]
        for bit in range(5):
            step = 1 << bit
            for low in range(HAD):
                if low & step:
                    continue
                first, second = values[low], values[low + step]
                values[low], values[low + step] = first + second, first - second
        for source in range(HAD):
            mixed[source, rows, :] = values[source]
        return 0

    lax.fori_loop(0, LIST_ROW // 8, butterfly, 0)
    for high in range(4):
        received = [pieces[high * 8 + low, LIST_ROW:PIECE, :] for low in range(8)]
        for low, value in enumerate(swap_segments(received)):
            lists[low, :, high * LANES : (high + 1) * LANES] = value

    def source_group(group, _):
        for low in range(8):
            source = group * 8 + low
            rows = lists[low, pl.ds(group, 1), :].astype(jnp.int32)
            fine = signs(jnp.bitwise_and(rows, 31), 32).astype(jnp.bfloat16)
            coarse = signs(jnp.right_shift(rows, 5), 32).astype(jnp.bfloat16)
            for step in range(32):
                table[low % 2, step * 32 : (step + 1) * 32, :] = fine * coarse[step : step + 1, :]
            main = jnp.concatenate([mixed[source, t * 32 : (t + 1) * 32, :] for t in range(8)], axis=1)
            tail = mixed[source, 256:272, :]
            tail = jnp.concatenate([tail[2 * t : 2 * t + 2, :] for t in range(8)], axis=1)
            main_high = main.astype(jnp.bfloat16).astype(jnp.float32)
            tail_high = tail.astype(jnp.bfloat16).astype(jnp.float32)
            left = jnp.concatenate(
                [
                    main_high,
                    main - main_high,
                    tail_high,
                    tail - tail_high,
                    jnp.zeros((4, ROWS), jnp.float32),
                ],
                axis=0,
            ).astype(jnp.bfloat16)
            product = jnp.dot(left, table[low % 2], preferred_element_type=jnp.float32)
            picked[low, 0:32, :] = (product[0:32] + product[32:64]) * scale
            picked[low, 32:34, :] = (product[64:66] + product[66:68]) * scale
        for high in range(4):
            lanes = slice(high * LANES, (high + 1) * LANES)
            moved = swap_segments([picked[low, :, lanes] for low in range(8)])
            for low, value in enumerate(moved):
                out[high * 8 + low, pl.ds(pl.multiple_of(group * 32, 32), 32), :] = value[0:32]
                extra[group, high * 8 + low] = value[32:40]
        return 0

    lax.fori_loop(0, 4, source_group, 0)
    for group in range(4):
        for owner in range(HAD):
            out[owner, 128 + 2 * group : 130 + 2 * group, :] = extra[group, owner, 0:2, :]


def gram_kernel(slot_total, received, live, gram, sketch, flipped):
    for group in range(4):
        lanes = slice(group * LANES, (group + 1) * LANES)
        keep = live[group : group + 1, :] > 0
        part = received[:, group * 32 : (group + 1) * 32, :].reshape(D, LANES)
        part = jnp.where(keep, part, 0.0)
        flipped[0:D, lanes] = part * (1.0 / slot_total)
        sketch[lanes, :] = part.T
        for half in range(2):
            for device in range(HAD):
                row = D + 32 * half + device
                source = 128 + 2 * group + half
                value = received[device, source : source + 1, :]
                flipped[row : row + 1, lanes] = jnp.where(keep, value, 0.0) * (1.0 / slot_total)
    for pair in range(BLOCKS // 2):
        first = 256 * pair
        block = jnp.dot(
            flipped[first:, :],
            sketch[:, first : first + 256],
            precision=HIGHEST,
            preferred_element_type=jnp.float32,
        )
        left, right = 2 * pair, 2 * pair + 1
        gram[COLUMN_START[left] : COLUMN_START[left] + COLUMN_ROWS[left], :] = block[:, :BLOCK]
        gram[COLUMN_START[right] : COLUMN_START[right] + COLUMN_ROWS[right], :] = block[BLOCK:, BLOCK:]


def across_lanes(value, lane):
    return jnp.broadcast_to(value[:, lane : lane + 1], value.shape)


def down_rows(value, row):
    return jnp.broadcast_to(value[row : row + 1, :], value.shape)


def inverse_factor(block):
    rows = [block[8 * g : 8 * g + 8, :] for g in range(16)]
    sub = lax.broadcasted_iota(jnp.int32, (8, LANES), 0)
    lane = lax.broadcasted_iota(jnp.int32, (8, LANES), 1)
    result = []
    for g in range(16):
        own = jnp.right_shift(lane, 3) == g
        columns = [across_lanes(rows[g], 8 * g + k) for k in range(8)]
        value = jnp.where(own, jnp.where(lane == 8 * g + sub, 1.0, 0.0), rows[g])
        finished = jnp.zeros((8, LANES), jnp.float32)
        for i in range(8):
            here = sub == i
            weight = columns[i]
            pivot = down_rows(weight, i)
            inverse = 1.0 / pivot
            root = lax.rsqrt(pivot)
            root = root * (1.5 - 0.5 * pivot * root * root)
            row = down_rows(value, i)
            finished = jnp.where(here, row * root, finished)

            def eliminate(held, entry):
                return jnp.where(here, 0.0, held) - jnp.where(here, -entry, weight * entry) * inverse

            value = eliminate(value, row)
            for k in range(i + 1, 8):
                columns[k] = eliminate(columns[k], down_rows(columns[k], i))
        result.append(jnp.where(lane <= 8 * g + sub, finished, 0.0))
        solved = [down_rows(value, k) for k in range(8)]
        far = min(16, g + 1 + NEAR_ROWS)
        for h in range(g + 1, far):
            terms = [across_lanes(rows[h], 8 * g + k) * solved[k] for k in range(8)]
            while len(terms) > 1:
                terms = [terms[t] + terms[t + 1] for t in range(0, len(terms), 2)]
            rows[h] = jnp.where(own, 0.0, rows[h]) - terms[0]
        if far < 16:
            left = jnp.concatenate([jnp.where(own, rows[h], 0.0) for h in range(far, 16)], axis=0)
            right = [value, jnp.zeros((LANES - 8 * g - 8, LANES), jnp.float32)]
            if g > 0:
                right.insert(0, jnp.zeros((8 * g, LANES), jnp.float32))
            change = times(left, jnp.concatenate(right, axis=0))
            for h in range(far, 16):
                rows[h] = jnp.where(own, 0.0, rows[h]) - change[8 * (h - far) : 8 * (h - far) + 8, :]
        yield result


def times_transposed(left, right):
    return lax.dot_general(
        left,
        right,
        (((1,), (1,)), ((), ())),
        precision=HIGHEST,
        preferred_element_type=jnp.float32,
    )


def times(left, right):
    return jnp.dot(left, right, precision=HIGHEST, preferred_element_type=jnp.float32)


def halves(value):
    high = value.astype(jnp.bfloat16)
    return high, (value - high.astype(jnp.float32)).astype(jnp.bfloat16)


def times_by_parts(left, right):
    left_high, left_low = halves(left)
    right_high, right_low = halves(right)
    return jnp.dot(
        jnp.concatenate([left_high, left_high, left_low], axis=1),
        jnp.concatenate([right_high, right_low, right_high], axis=0),
        preferred_element_type=jnp.float32,
    )


def beside(steps, tasks, watch):
    tasks, left = list(tasks), 16
    while True:
        try:
            seen = next(steps)
        except StopIteration:
            return jnp.concatenate(seen, axis=0)
        for _ in range(-(-len(tasks) // left)):
            tasks.pop(0)()
        watch(seen)
        left = max(left - 1, 1)


def solve_kernel(gram, sketch, basis, coefficients, lower, inverted, flipped, answer):
    row = lax.broadcasted_iota(jnp.int32, (BLOCK, BLOCK), 0)
    column = lax.broadcasted_iota(jnp.int32, (BLOCK, BLOCK), 1)
    ridge = jnp.where(row == column, RIDGE, 0.0)

    def at(i, j, end=None):
        start = COLUMN_START[j] + BLOCK * (i - j)
        last = COLUMN_START[j] + (COLUMN_ROWS[j] if end == 9 else BLOCK * ((i if end is None else end) + 1 - j))
        return slice(start, last)

    def pieces_of(first, alone=True):
        pieces = [(first, first)] if alone and first < BLOCKS - 1 else []
        first += len(pieces)
        while first < BLOCKS:
            last = min(first + 1, BLOCKS - 1)
            pieces.append((first, 9 if last == BLOCKS - 1 else last))
            first = last + 1
        return pieces or [(BLOCKS, 9)]

    def copy_task(j):
        def task():
            lower[at(j, j), :] = gram[at(j, j), :] + ridge
            rest = at(j + 1, j, 9)
            lower[rest, :] = gram[rest, :]

        return task

    def panel_tasks(k, upright):
        def rows_task(first, last):
            def task():
                rows = at(first, k, last)
                lower[rows, :] = times(lower[rows, :], upright)

            return task

        def sketch_task(part):
            def task():
                rows = slice(BLOCK * part, BLOCK * (part + 1))
                own = slice(BLOCK * k, BLOCK * (k + 1))
                source = sketch if k == 0 else basis
                basis[rows, own] = times_by_parts(source[rows, own], upright)

            return task

        return [rows_task(*piece) for piece in pieces_of(k + 2)], [sketch_task(part) for part in range(4)]

    def near_tasks(k, upright):
        def rows_task(first, last):
            def task():
                rows = at(first, k + 1, last)
                lower[rows, :] = lower[rows, :] - times(lower[at(first, k, last), :], upright)

            return task

        def corner_task():
            value = lower[at(k + 2, k), :]
            rows = at(k + 2, k + 2)
            lower[rows, :] = lower[rows, :] - times_transposed(value, value)

        def sketch_task(part):
            def task():
                rows = slice(BLOCK * part, BLOCK * (part + 1))
                own = slice(BLOCK * k, BLOCK * (k + 1))
                beyond = slice(BLOCK * (k + 1), BLOCK * (k + 2))
                source = sketch if k < 2 else basis
                basis[rows, beyond] = source[rows, beyond] - times_by_parts(basis[rows, own], upright)

            return task

        above = [rows_task(*piece) for piece in pieces_of(k + 2)]
        if k + 2 < BLOCKS:
            above.append(corner_task)
        return above, [sketch_task(part) for part in range(4)]

    def wide(first, last, k):
        return jnp.concatenate([lower[at(first, k - 1, last), :], lower[at(first, k, last), :]], axis=1)

    def far_tasks(k):
        above, below = [], []

        def flip_task(c):
            def task():
                flipped[:, BLOCK * c : BLOCK * (c + 2)] = wide(c, c + 1, k).T

            return task

        def rows_task(c, first, last):
            def task():
                change = times(wide(first, last, k), flipped[:, BLOCK * c : BLOCK * (c + 2)])
                if first == c:
                    if c > k + 1:
                        rows = at(c, c)
                        lower[rows, :] = lower[rows, :] - change[:BLOCK, :BLOCK]
                    rows = at(c + 1, c)
                    lower[rows, :] = lower[rows, :] - change[BLOCK : 2 * BLOCK, :BLOCK]
                    rows = at(c + 1, c + 1)
                    lower[rows, :] = lower[rows, :] - change[BLOCK : 2 * BLOCK, BLOCK:]
                    if last == 9:
                        for half in range(2):
                            rows = at(BLOCKS, c + half, 9)
                            lanes = slice(BLOCK * half, BLOCK * (half + 1))
                            lower[rows, :] = lower[rows, :] - change[2 * BLOCK :, lanes]
                else:
                    for half in range(2):
                        rows = at(first, c + half, last)
                        lanes = slice(BLOCK * half, BLOCK * (half + 1))
                        lower[rows, :] = lower[rows, :] - change[:, lanes]

            return task

        def sketch_task(c, part):
            def task():
                rows = slice(BLOCK * part, BLOCK * (part + 1))
                own = slice(BLOCK * (k - 1), BLOCK * (k + 1))
                beyond = slice(BLOCK * c, BLOCK * (c + 2))
                source = sketch if k < 2 else basis
                basis[rows, beyond] = source[rows, beyond] - times_by_parts(basis[rows, own], flipped[:, beyond])

            return task

        for c in range(k + 1, BLOCKS, 2):
            above.append(flip_task(c))
            above += [rows_task(c, *piece) for piece in pieces_of(c, False)]
            below += [sketch_task(c, part) for part in range(4)]
        return above, below

    def inverse_tasks(k, inverse):
        own = slice(BLOCK * k, BLOCK * (k + 1))

        def finish_task():
            if k > 0:
                inverted[own, : BLOCK * k] = -times_by_parts(inverse, inverted[own, : BLOCK * k])
            inverted[own, own] = inverse
            if k % 2 == 0:
                inverted[own, BLOCK * (k + 1) : BLOCK * (k + 2)] = jnp.zeros((BLOCK, BLOCK), jnp.float32)

        def answer_task():
            change = times_by_parts(lower[at(BLOCKS, k, 9), :], inverted[own, : BLOCK * (k + 1)])
            if k > 0:
                answer[:, : BLOCK * k] = answer[:, : BLOCK * k] + change[:, : BLOCK * k]
            answer[:, own] = change[:, BLOCK * k :]

        def next_task(first):
            def task():
                rows = slice(BLOCK * first, BLOCK * (k + 1))
                columns = slice(BLOCK * first, BLOCK * min(first + 2, k + 1))
                left = jnp.concatenate([lower[at(k + 1, j), :] for j in range(first, k + 1)], axis=1)
                inverted[BLOCK * (k + 1) : BLOCK * (k + 2), columns] = times_by_parts(left, inverted[rows, columns])

            return task

        return [finish_task, answer_task] + [next_task(first) for first in range(0, k + 1 if k + 1 < BLOCKS else 0, 2)]

    for j in range(BLOCKS):
        copy_task(j)()
    for k in range(BLOCKS):
        own = slice(BLOCK * k, BLOCK * (k + 1))
        block = lower[at(k, k), :]
        if k < BLOCKS - 1:
            beyond = lower[at(k + 1, k), :].T
        else:
            beyond = None

        def watch(seen):
            if k < BLOCKS - 1 and len(seen) in RUN_ENDS:
                part = times(jnp.concatenate(seen[RUN_ENDS[len(seen)] :], axis=0), beyond)
                next_upright.append(part)
                changes.append(times(part.T, part))
            if k < BLOCKS - 1 and len(seen) == 16:
                change = changes[0]
                for more in changes[1:-1]:
                    change = change + more
                corner = at(k + 1, k + 1)
                lower[corner, :] = (lower[corner, :] - change) - changes[-1]

        changes, next_upright = [], []
        inverse = beside(inverse_factor(block), tasks if k else [], watch)
        upright = inverse.T
        if k < BLOCKS - 1:
            value_upright = jnp.concatenate(next_upright, axis=0)
            lower[at(k + 1, k), :] = value_upright.T
        above, below = panel_tasks(k, upright)
        if k == BLOCKS - 1:
            more_above, more_below = [], []
        elif k % 2 == 0:
            more_above, more_below = near_tasks(k, value_upright)
        else:
            more_above, more_below = far_tasks(k)
        extra = inverse_tasks(k, inverse)
        if k == BLOCKS - 1:
            tasks = above + extra + below
        else:
            early = above[:1] + (more_above[:1] if k % 2 == 0 else more_above[:2])
            for task in early:
                task()
            tasks = above[1:] + more_above[len(early) - 1 :] + below + extra + more_below
    for task in tasks:
        task()
    coefficients[...] = answer[...].T


def swap_cores(value):
    return lax.ppermute(value, "had", [(device, device ^ 1) for device in range(HAD)])


SOLVE_SCRATCH = [
    pltpu.VMEM((PACKED, LANES), jnp.float32),
    pltpu.VMEM((D, D), jnp.float32),
    pltpu.VMEM((2 * BLOCK, D), jnp.float32),
    pltpu.VMEM((K, D), jnp.float32),
]


def total(gram):
    core = jnp.bitwise_and(lax.axis_index("had"), 1)
    half = PACKED // 2
    mine = lax.dynamic_slice_in_dim(gram, core * half, half, 0)
    other = lax.dynamic_slice_in_dim(gram, (1 - core) * half, half, 0)
    part = mine + swap_cores(other)
    chips = [[2 * chip + own for chip in range(HAD // 2)] for own in range(2)]
    part = part.reshape(HAD // 2, half // (HAD // 2), LANES)
    part = lax.all_to_all(part, "had", 0, 0, tiled=True, axis_index_groups=chips)
    part = jnp.sum(part, axis=0)
    size = lax.axis_size("grp")
    part = jnp.broadcast_to(part[None], (size, *part.shape))
    part = jnp.sum(lax.all_to_all(part, "grp", 0, 0, tiled=True), axis=0)
    part = jnp.broadcast_to(part[None], (HAD // 2, *part.shape))
    part = lax.all_to_all(part, "had", 0, 0, tiled=True, axis_index_groups=chips)
    part = part.reshape(half, LANES)
    other = swap_cores(part)
    first = jnp.where(core == 0, part, other)
    second = jnp.where(core == 0, other, part)
    return jnp.concatenate([first, second], axis=0)


def on_device(embeddings, targets, sign_bits, samples, counts):
    had_size = lax.axis_size("had")
    factor = (1 - 2 * sign_bits).astype(jnp.float32).reshape(8, LANES)
    lists = samples.reshape(4, LANES).astype(jnp.float32)
    pieces = call(spread_kernel, f32(HAD, PIECE, LANES), [], 40, embeddings, targets, factor, lists)
    pieces = lax.all_to_all(pieces, "had", split_axis=0, concat_axis=0, tiled=True)
    outgoing = call(
        mix_kernel,
        f32(HAD, BACK, LANES),
        [
            pltpu.VMEM((HAD, LIST_ROW, LANES), jnp.float32),
            pltpu.VMEM((8, 8, SLOTS), jnp.float32),
            pltpu.VMEM((2, ROWS, SLOTS), jnp.bfloat16),
            pltpu.VMEM((8, 40, SLOTS), jnp.float32),
            pltpu.VMEM((4, HAD, 8, LANES), jnp.float32),
        ],
        40,
        pieces,
    )
    received = lax.all_to_all(outgoing, "had", split_axis=0, concat_axis=0, tiled=True)
    slot = jnp.arange(CAP, dtype=jnp.int32)[None, :]
    live = (slot < counts.reshape(had_size)[:, None]).astype(jnp.float32).reshape(4, LANES)
    slot_total = lax.axis_size("grp") * had_size * SLOTS
    gram, sketch = call(
        lambda *refs: gram_kernel(slot_total, *refs),
        (f32(PACKED, LANES), f32(SLOTS, D)),
        [pltpu.VMEM((D + K, SLOTS), jnp.float32)],
        40,
        received,
        live,
    )
    gram = total(gram)
    return call(solve_kernel, (f32(SLOTS, D), f32(D, K)), SOLVE_SCRATCH, 40, gram, sketch)


def solution(mesh):
    placed = (
        P(("grp", "had"), None),
        P(("grp", "had"), None),
        P(("grp", "had")),
        P(("grp", "had"), None, None),
        P(("grp", "had"), None),
    )
    return jax.shard_map(
        on_device,
        mesh=mesh,
        in_specs=placed,
        out_specs=(P(("grp", "had"), None), P()),
        check_vma=False,
    )
```

```python
import math

import jax
import jax.numpy as jnp
from jax import lax
from jax.experimental import pallas as pl
from jax.experimental.pallas import tpu as pltpu
from jax.sharding import PartitionSpec as P

D = 1024
K = 64
CAP = 16
HAD = 32
ROWS = 1024
SLOTS = 512
LANES = 128
BLOCK = 128
BLOCKS = D // BLOCK
RIDGE = 0.05
BOTH = ("grp", "had")

PIECE = 280
LIST_ROW = 272
BACK = 136
HIGHEST = lax.Precision.HIGHEST
COLUMN_ROWS = [D + K - BLOCK * j for j in range(BLOCKS)]
COLUMN_START = [sum(COLUMN_ROWS[:j]) for j in range(BLOCKS)]
PACKED = sum(COLUMN_ROWS)
MIB = 1024 * 1024
NEAR_ROWS = 2
RUN_ENDS = {8: 0, 12: 8, 16: 12}


def call(kernel, out_shape, scratch, vmem_mib, *args, scalars=0):
    spaces = [pltpu.VMEM] * (len(args) - scalars) + [pltpu.SMEM] * scalars
    return pl.pallas_call(
        kernel,
        out_shape=out_shape,
        in_specs=[pl.BlockSpec(memory_space=space) for space in spaces],
        out_specs=jax.tree.map(lambda _: pl.BlockSpec(memory_space=pltpu.VMEM), out_shape),
        scratch_shapes=scratch,
        compiler_params=pltpu.CompilerParams(vmem_limit_bytes=vmem_mib * MIB),
    )(*args)


def f32(*shape):
    return jax.ShapeDtypeStruct(shape, jnp.float32)


def spread_kernel(embeddings, targets, sign_bits, lists, out):
    factor = (1 - 2 * sign_bits[...]).astype(jnp.float32)
    for tile in range(8):
        rows = slice(tile * LANES, (tile + 1) * LANES)
        sign = factor[tile : tile + 1, :]
        columns = embeddings[rows, :].astype(jnp.float32).T * sign
        out[:, tile * 32 : (tile + 1) * 32, :] = columns.reshape(HAD, 32, LANES)
        extra = targets[:, rows].astype(jnp.float32) * sign
        for device in range(HAD):
            for half in range(2):
                row = 256 + 2 * tile + half
                source = 32 * half + device
                out[device, row : row + 1, :] = extra[source : source + 1, :]
    tail = jnp.concatenate([lists[...].astype(jnp.float32), jnp.zeros((4, LANES), jnp.float32)], axis=0)
    out[:, LIST_ROW:PIECE, :] = jnp.broadcast_to(tail[None], (HAD, 8, LANES))


def swap_segments(values):
    values = list(values)
    lane = lax.broadcasted_iota(jnp.int32, values[0].shape, values[0].ndim - 1)
    for bit in range(3):
        step = 1 << bit
        upper = jnp.bitwise_and(jnp.right_shift(lane, 4 + bit), 1) == 1
        for low in range(8):
            if low & step:
                continue
            first, second = values[low], values[low + step]
            values[low] = jnp.where(upper, pltpu.roll(second, 16 * step, 1), first)
            values[low + step] = jnp.where(upper, second, pltpu.roll(first, LANES - 16 * step, 1))
    return values


def signs(row_bits, count):
    both = jnp.bitwise_and(lax.broadcasted_iota(jnp.int32, (count, row_bits.shape[1]), 0), row_bits)
    for shift in (4, 2, 1):
        both = jnp.bitwise_xor(both, jnp.right_shift(both, shift))
    return (1 - 2 * jnp.bitwise_and(both, 1)).astype(jnp.float32)


def mix_kernel(pieces, out, mixed, lists, table, picked, extra):
    scale = 1.0 / math.sqrt(ROWS * HAD)

    def butterfly(chunk, _):
        rows = pl.ds(pl.multiple_of(chunk * 8, 8), 8)
        values = [pieces[device, rows, :] for device in range(HAD)]
        for bit in range(5):
            step = 1 << bit
            for low in range(HAD):
                if low & step:
                    continue
                first, second = values[low], values[low + step]
                values[low], values[low + step] = first + second, first - second
        for source in range(HAD):
            mixed[source, rows, :] = values[source]
        return 0

    lax.fori_loop(0, LIST_ROW // 8, butterfly, 0)
    for high in range(4):
        received = [pieces[high * 8 + low, LIST_ROW:PIECE, :] for low in range(8)]
        for low, value in enumerate(swap_segments(received)):
            lists[low, :, high * LANES : (high + 1) * LANES] = value

    def source_group(group, _):
        for low in range(8):
            source = group * 8 + low
            rows = lists[low, pl.ds(group, 1), :].astype(jnp.int32)
            fine = signs(jnp.bitwise_and(rows, 31), 32).astype(jnp.bfloat16)
            coarse = signs(jnp.right_shift(rows, 5), 32).astype(jnp.bfloat16)
            for step in range(32):
                table[low % 2, step * 32 : (step + 1) * 32, :] = fine * coarse[step : step + 1, :]
            main = jnp.concatenate([mixed[source, t * 32 : (t + 1) * 32, :] for t in range(8)], axis=1)
            tail = mixed[source, 256:272, :]
            tail = jnp.concatenate([tail[2 * t : 2 * t + 2, :] for t in range(8)], axis=1)
            main_high = main.astype(jnp.bfloat16).astype(jnp.float32)
            tail_high = tail.astype(jnp.bfloat16).astype(jnp.float32)
            left = jnp.concatenate(
                [
                    main_high,
                    main - main_high,
                    tail_high,
                    tail - tail_high,
                    jnp.zeros((4, ROWS), jnp.float32),
                ],
                axis=0,
            ).astype(jnp.bfloat16)
            product = jnp.dot(left, table[low % 2], preferred_element_type=jnp.float32)
            picked[low, 0:32, :] = (product[0:32] + product[32:64]) * scale
            picked[low, 32:34, :] = (product[64:66] + product[66:68]) * scale
        for high in range(4):
            lanes = slice(high * LANES, (high + 1) * LANES)
            moved = swap_segments([picked[low, :, lanes] for low in range(8)])
            for low, value in enumerate(moved):
                out[high * 8 + low, pl.ds(pl.multiple_of(group * 32, 32), 32), :] = value[0:32]
                extra[group, high * 8 + low] = value[32:40]
        return 0

    lax.fori_loop(0, 4, source_group, 0)
    for group in range(4):
        for owner in range(HAD):
            out[owner, 128 + 2 * group : 130 + 2 * group, :] = extra[group, owner, 0:2, :]


def gram_kernel(slot_total, received, counts, gram, sketch, flipped):
    lane = lax.broadcasted_iota(jnp.int32, (1, LANES), 1)
    segment, slot = jnp.right_shift(lane, 4), jnp.bitwise_and(lane, CAP - 1)
    for group in range(4):
        lanes = slice(group * LANES, (group + 1) * LANES)
        live = jnp.zeros((1, LANES), jnp.int32)
        for low in range(8):
            live = jnp.where(segment == low, counts[0, 8 * group + low], live)
        keep = slot < live
        part = received[:, group * 32 : (group + 1) * 32, :].reshape(D, LANES)
        part = jnp.where(keep, part, 0.0)
        flipped[0:D, lanes] = part * (1.0 / slot_total)
        sketch[lanes, :] = part.T
        for half in range(2):
            for device in range(HAD):
                row = D + 32 * half + device
                source = 128 + 2 * group + half
                value = received[device, source : source + 1, :]
                flipped[row : row + 1, lanes] = jnp.where(keep, value, 0.0) * (1.0 / slot_total)
    for pair in range(BLOCKS // 2):
        first = 256 * pair
        block = times_by_parts(flipped[first:, :], sketch[:, first : first + 256])
        left, right = 2 * pair, 2 * pair + 1
        gram[COLUMN_START[left] : COLUMN_START[left] + COLUMN_ROWS[left], :] = block[:, :BLOCK]
        gram[COLUMN_START[right] : COLUMN_START[right] + COLUMN_ROWS[right], :] = block[BLOCK:, BLOCK:]


def across_lanes(value, lane):
    return jnp.broadcast_to(value[:, lane : lane + 1], value.shape)


def down_rows(value, row):
    return jnp.broadcast_to(value[row : row + 1, :], value.shape)


def inverse_factor(block):
    rows = [block[8 * g : 8 * g + 8, :] for g in range(16)]
    sub = lax.broadcasted_iota(jnp.int32, (8, LANES), 0)
    lane = lax.broadcasted_iota(jnp.int32, (8, LANES), 1)
    result = []
    for g in range(16):
        own = jnp.right_shift(lane, 3) == g
        columns = [across_lanes(rows[g], 8 * g + k) for k in range(8)]
        value = jnp.where(own, jnp.where(lane == 8 * g + sub, 1.0, 0.0), rows[g])
        finished = jnp.zeros((8, LANES), jnp.float32)
        for i in range(8):
            here = sub == i
            weight = columns[i]
            pivot = down_rows(weight, i)
            inverse = 1.0 / pivot
            root = lax.rsqrt(pivot)
            root = root * (1.5 - 0.5 * pivot * root * root)
            row = down_rows(value, i)
            finished = jnp.where(here, row * root, finished)

            def eliminate(held, entry):
                return jnp.where(here, 0.0, held) - jnp.where(here, -entry, weight * entry) * inverse

            value = eliminate(value, row)
            for k in range(i + 1, 8):
                columns[k] = eliminate(columns[k], down_rows(columns[k], i))
        result.append(jnp.where(lane <= 8 * g + sub, finished, 0.0))
        solved = [down_rows(value, k) for k in range(8)]
        far = min(16, g + 1 + NEAR_ROWS)
        for h in range(g + 1, far):
            terms = [across_lanes(rows[h], 8 * g + k) * solved[k] for k in range(8)]
            while len(terms) > 1:
                terms = [terms[t] + terms[t + 1] for t in range(0, len(terms), 2)]
            rows[h] = jnp.where(own, 0.0, rows[h]) - terms[0]
        if far < 16:
            left = jnp.concatenate([jnp.where(own, rows[h], 0.0) for h in range(far, 16)], axis=0)
            right = [value, jnp.zeros((LANES - 8 * g - 8, LANES), jnp.float32)]
            if g > 0:
                right.insert(0, jnp.zeros((8 * g, LANES), jnp.float32))
            change = times(left, jnp.concatenate(right, axis=0))
            for h in range(far, 16):
                rows[h] = jnp.where(own, 0.0, rows[h]) - change[8 * (h - far) : 8 * (h - far) + 8, :]
        yield result


def times_transposed(left, right):
    return lax.dot_general(
        left,
        right,
        (((1,), (1,)), ((), ())),
        precision=HIGHEST,
        preferred_element_type=jnp.float32,
    )


def times(left, right):
    return jnp.dot(left, right, precision=HIGHEST, preferred_element_type=jnp.float32)


def halves(value):
    high = value.astype(jnp.bfloat16)
    return high, (value - high.astype(jnp.float32)).astype(jnp.bfloat16)


def times_by_parts(left, right):
    left_high, left_low = halves(left)
    right_high, right_low = halves(right)
    return jnp.dot(
        jnp.concatenate([left_high, left_high, left_low], axis=1),
        jnp.concatenate([right_high, right_low, right_high], axis=0),
        preferred_element_type=jnp.float32,
    )


def beside(steps, tasks, watch):
    tasks, left = list(tasks), 16
    while True:
        try:
            seen = next(steps)
        except StopIteration:
            return jnp.concatenate(seen, axis=0)
        for _ in range(-(-len(tasks) // left)):
            tasks.pop(0)()
        watch(seen)
        left = max(left - 1, 1)


def solve_kernel(gram, sketch, basis, answer, lower, inverted, flipped):
    row = lax.broadcasted_iota(jnp.int32, (BLOCK, BLOCK), 0)
    column = lax.broadcasted_iota(jnp.int32, (BLOCK, BLOCK), 1)
    ridge = jnp.where(row == column, RIDGE, 0.0)

    def at(i, j, end=None):
        start = COLUMN_START[j] + BLOCK * (i - j)
        last = COLUMN_START[j] + (COLUMN_ROWS[j] if end == 9 else BLOCK * ((i if end is None else end) + 1 - j))
        return slice(start, last)

    def pieces_of(first, alone=True):
        pieces = [(first, first)] if alone and first < BLOCKS - 1 else []
        first += len(pieces)
        while first < BLOCKS:
            last = min(first + 1, BLOCKS - 1)
            pieces.append((first, 9 if last == BLOCKS - 1 else last))
            first = last + 1
        return pieces or [(BLOCKS, 9)]

    def copy_task(j):
        def task():
            lower[at(j, j), :] = gram[at(j, j), :] + ridge
            rest = at(j + 1, j, 9)
            lower[rest, :] = gram[rest, :]

        return task

    def panel_tasks(k, upright):
        def rows_task(first, last):
            def task():
                rows = at(first, k, last)
                lower[rows, :] = times(lower[rows, :], upright)

            return task

        def sketch_task(part):
            def task():
                rows = slice(BLOCK * part, BLOCK * (part + 1))
                own = slice(BLOCK * k, BLOCK * (k + 1))
                source = sketch if k == 0 else basis
                basis[rows, own] = times_by_parts(source[rows, own], upright)

            return task

        return [rows_task(*piece) for piece in pieces_of(k + 2)], [sketch_task(part) for part in range(4)]

    def near_tasks(k, upright):
        def rows_task(first, last):
            def task():
                rows = at(first, k + 1, last)
                lower[rows, :] = lower[rows, :] - times(lower[at(first, k, last), :], upright)

            return task

        def corner_task():
            value = lower[at(k + 2, k), :]
            rows = at(k + 2, k + 2)
            lower[rows, :] = lower[rows, :] - times_transposed(value, value)

        def sketch_task(part):
            def task():
                rows = slice(BLOCK * part, BLOCK * (part + 1))
                own = slice(BLOCK * k, BLOCK * (k + 1))
                beyond = slice(BLOCK * (k + 1), BLOCK * (k + 2))
                source = sketch if k < 2 else basis
                basis[rows, beyond] = source[rows, beyond] - times_by_parts(basis[rows, own], upright)

            return task

        above = [rows_task(*piece) for piece in pieces_of(k + 2)]
        if k + 2 < BLOCKS:
            above.append(corner_task)
        return above, [sketch_task(part) for part in range(4)]

    def wide(first, last, k):
        return jnp.concatenate([lower[at(first, k - 1, last), :], lower[at(first, k, last), :]], axis=1)

    def far_tasks(k):
        above, below = [], []

        def flip_task(c):
            def task():
                flipped[:, BLOCK * c : BLOCK * (c + 2)] = wide(c, c + 1, k).T

            return task

        def rows_task(c, first, last):
            def task():
                change = times(wide(first, last, k), flipped[:, BLOCK * c : BLOCK * (c + 2)])
                if first == c:
                    if c > k + 1:
                        rows = at(c, c)
                        lower[rows, :] = lower[rows, :] - change[:BLOCK, :BLOCK]
                    rows = at(c + 1, c)
                    lower[rows, :] = lower[rows, :] - change[BLOCK : 2 * BLOCK, :BLOCK]
                    rows = at(c + 1, c + 1)
                    lower[rows, :] = lower[rows, :] - change[BLOCK : 2 * BLOCK, BLOCK:]
                    if last == 9:
                        for half in range(2):
                            rows = at(BLOCKS, c + half, 9)
                            lanes = slice(BLOCK * half, BLOCK * (half + 1))
                            lower[rows, :] = lower[rows, :] - change[2 * BLOCK :, lanes]
                else:
                    for half in range(2):
                        rows = at(first, c + half, last)
                        lanes = slice(BLOCK * half, BLOCK * (half + 1))
                        lower[rows, :] = lower[rows, :] - change[:, lanes]

            return task

        def sketch_task(c, part):
            def task():
                rows = slice(BLOCK * part, BLOCK * (part + 1))
                own = slice(BLOCK * (k - 1), BLOCK * (k + 1))
                beyond = slice(BLOCK * c, BLOCK * (c + 2))
                source = sketch if k < 2 else basis
                basis[rows, beyond] = source[rows, beyond] - times_by_parts(basis[rows, own], flipped[:, beyond])

            return task

        for c in range(k + 1, BLOCKS, 2):
            above.append(flip_task(c))
            above += [rows_task(c, *piece) for piece in pieces_of(c, False)]
            below += [sketch_task(c, part) for part in range(4)]
        return above, below

    def inverse_tasks(k, inverse):
        own = slice(BLOCK * k, BLOCK * (k + 1))

        def finish_task():
            if k > 0:
                inverted[own, : BLOCK * k] = -times_by_parts(inverse, inverted[own, : BLOCK * k])
            inverted[own, own] = inverse
            if k % 2 == 0:
                inverted[own, BLOCK * (k + 1) : BLOCK * (k + 2)] = jnp.zeros((BLOCK, BLOCK), jnp.float32)

        def answer_task():
            change = times_by_parts(lower[at(BLOCKS, k, 9), :], inverted[own, : BLOCK * (k + 1)])
            if k > 0:
                answer[:, : BLOCK * k] = answer[:, : BLOCK * k] + change[:, : BLOCK * k]
            answer[:, own] = change[:, BLOCK * k :]

        def next_task(first):
            def task():
                rows = slice(BLOCK * first, BLOCK * (k + 1))
                columns = slice(BLOCK * first, BLOCK * min(first + 2, k + 1))
                left = jnp.concatenate([lower[at(k + 1, j), :] for j in range(first, k + 1)], axis=1)
                inverted[BLOCK * (k + 1) : BLOCK * (k + 2), columns] = times_by_parts(left, inverted[rows, columns])

            return task

        return [finish_task, answer_task] + [next_task(first) for first in range(0, k + 1 if k + 1 < BLOCKS else 0, 2)]

    for j in range(BLOCKS):
        copy_task(j)()
    for k in range(BLOCKS):
        own = slice(BLOCK * k, BLOCK * (k + 1))
        block = lower[at(k, k), :]
        if k < BLOCKS - 1:
            beyond = lower[at(k + 1, k), :].T
        else:
            beyond = None

        def watch(seen):
            if k < BLOCKS - 1 and len(seen) in RUN_ENDS:
                part = times(jnp.concatenate(seen[RUN_ENDS[len(seen)] :], axis=0), beyond)
                next_upright.append(part)
                changes.append(times(part.T, part))
            if k < BLOCKS - 1 and len(seen) == 16:
                change = changes[0]
                for more in changes[1:-1]:
                    change = change + more
                corner = at(k + 1, k + 1)
                lower[corner, :] = (lower[corner, :] - change) - changes[-1]

        changes, next_upright = [], []
        inverse = beside(inverse_factor(block), tasks if k else [], watch)
        upright = inverse.T
        if k < BLOCKS - 1:
            value_upright = jnp.concatenate(next_upright, axis=0)
            lower[at(k + 1, k), :] = value_upright.T
        above, below = panel_tasks(k, upright)
        if k == BLOCKS - 1:
            more_above, more_below = [], []
        elif k % 2 == 0:
            more_above, more_below = near_tasks(k, value_upright)
        else:
            more_above, more_below = far_tasks(k)
        extra = inverse_tasks(k, inverse)
        if k == BLOCKS - 1:
            tasks = above + extra + below
        else:
            early = above[:1] + (more_above[:1] if k % 2 == 0 else more_above[:2])
            for task in early:
                task()
            tasks = above[1:] + more_above[len(early) - 1 :] + below + extra + more_below
    for task in tasks:
        task()


def swap_cores(value):
    return lax.ppermute(value, "had", [(device, device ^ 1) for device in range(HAD)])


SOLVE_SCRATCH = [
    pltpu.VMEM((PACKED, LANES), jnp.float32),
    pltpu.VMEM((D, D), jnp.float32),
    pltpu.VMEM((2 * BLOCK, D), jnp.float32),
]


def total(gram):
    core = jnp.bitwise_and(lax.axis_index("had"), 1)
    half = PACKED // 2
    mine = lax.dynamic_slice_in_dim(gram, core * half, half, 0)
    other = lax.dynamic_slice_in_dim(gram, (1 - core) * half, half, 0)
    part = mine + swap_cores(other)
    chips = [[2 * chip + own for chip in range(HAD // 2)] for own in range(2)]
    part = part.reshape(HAD // 2, half // (HAD // 2), LANES)
    part = lax.all_to_all(part, "had", 0, 0, tiled=True, axis_index_groups=chips)
    part = jnp.sum(part, axis=0)
    size = lax.axis_size("grp")
    part = jnp.broadcast_to(part[None], (size, *part.shape))
    part = jnp.sum(lax.all_to_all(part, "grp", 0, 0, tiled=True), axis=0)
    part = jnp.broadcast_to(part[None], (HAD // 2, *part.shape))
    part = lax.all_to_all(part, "had", 0, 0, tiled=True, axis_index_groups=chips)
    part = part.reshape(half, LANES)
    other = swap_cores(part)
    first = jnp.where(core == 0, part, other)
    second = jnp.where(core == 0, other, part)
    return jnp.concatenate([first, second], axis=0)


def on_device(embeddings, targets, sign_bits, samples, counts):
    had_size = lax.axis_size("had")
    lists = samples.reshape(4, LANES)
    pieces = call(
        spread_kernel, f32(HAD, PIECE, LANES), [], 12, embeddings, targets.T, sign_bits.reshape(8, LANES), lists
    )
    pieces = lax.all_to_all(pieces, "had", split_axis=0, concat_axis=0, tiled=True)
    outgoing = call(
        mix_kernel,
        f32(HAD, BACK, LANES),
        [
            pltpu.VMEM((HAD, LIST_ROW, LANES), jnp.float32),
            pltpu.VMEM((8, 8, SLOTS), jnp.float32),
            pltpu.VMEM((2, ROWS, SLOTS), jnp.bfloat16),
            pltpu.VMEM((8, 40, SLOTS), jnp.float32),
            pltpu.VMEM((4, HAD, 8, LANES), jnp.float32),
        ],
        20,
        pieces,
    )
    received = lax.all_to_all(outgoing, "had", split_axis=0, concat_axis=0, tiled=True)
    slot_total = lax.axis_size("grp") * had_size * SLOTS
    gram, sketch = call(
        lambda *refs: gram_kernel(slot_total, *refs),
        (f32(PACKED, LANES), f32(SLOTS, D)),
        [pltpu.VMEM((D + K, SLOTS), jnp.float32)],
        16,
        received,
        counts,
        scalars=1,
    )
    gram = total(gram)
    basis, coefficients = call(solve_kernel, (f32(SLOTS, D), f32(K, D)), SOLVE_SCRATCH, 20, gram, sketch)
    return basis, coefficients.T


def solution(mesh):
    placed = (
        P(("grp", "had"), None),
        P(("grp", "had"), None),
        P(("grp", "had")),
        P(("grp", "had"), None, None),
        P(("grp", "had"), None),
    )
    return jax.shard_map(
        on_device,
        mesh=mesh,
        in_specs=placed,
        out_specs=(P(("grp", "had"), None), P()),
        check_vma=False,
    )
```

```python
import math

import jax
import jax.numpy as jnp
from jax import lax
from jax.experimental import pallas as pl
from jax.experimental.pallas import tpu as pltpu
from jax.sharding import PartitionSpec as P

D = 1024
K = 64
CAP = 16
HAD = 32
ROWS = 1024
SLOTS = 512
LANES = 128
BLOCK = 128
BLOCKS = D // BLOCK
RIDGE = 0.05
BOTH = ("grp", "had")

PIECE = 280
LIST_ROW = 272
BACK = 136
HIGHEST = lax.Precision.HIGHEST
COLUMN_ROWS = [D + K - BLOCK * j for j in range(BLOCKS)]
COLUMN_START = [sum(COLUMN_ROWS[:j]) for j in range(BLOCKS)]
PACKED = sum(COLUMN_ROWS)
MIB = 1024 * 1024
NEAR_ROWS = 2
RUN_ENDS = {8: 0, 14: 8}
LAST_RUN = 14


def call(kernel, outs, scratch, vmem_mib, *args):
    return pl.pallas_call(
        kernel,
        out_shape=[shape for _, shape in outs],
        in_specs=[pl.BlockSpec(memory_space=space) for space, _ in args],
        out_specs=[pl.BlockSpec(memory_space=space) for space, _ in outs],
        scratch_shapes=scratch,
        compiler_params=pltpu.CompilerParams(vmem_limit_bytes=vmem_mib * MIB),
    )(*[array for _, array in args])


def f32(*shape):
    return jax.ShapeDtypeStruct(shape, jnp.float32)


def spread_kernel(embeddings_in, targets_in, sign_bits_in, lists, out, embeddings, targets, sign_bits, arrived):
    small = [
        pltpu.make_async_copy(sign_bits_in, sign_bits, arrived.at[0]),
        pltpu.make_async_copy(targets_in, targets, arrived.at[1]),
    ]
    large = []
    for part in range(4):
        rows = slice(part * 256, (part + 1) * 256)
        large.append(pltpu.make_async_copy(embeddings_in.at[rows, :], embeddings.at[rows, :], arrived.at[2 + part]))
    for copy in small + large:
        copy.start()
    for copy in small:
        copy.wait()
    factor = (1 - 2 * sign_bits[...]).astype(jnp.float32)
    for tile in range(8):
        if tile % 2 == 0:
            large[tile // 2].wait()
        rows = slice(tile * LANES, (tile + 1) * LANES)
        sign = factor[tile : tile + 1, :]
        columns = embeddings[rows, :].astype(jnp.float32).T * sign
        out[:, tile * 32 : (tile + 1) * 32, :] = columns.reshape(HAD, 32, LANES)
        extra = targets[:, rows].astype(jnp.float32) * sign
        for device in range(HAD):
            for half in range(2):
                row = 256 + 2 * tile + half
                source = 32 * half + device
                out[device, row : row + 1, :] = extra[source : source + 1, :]
    tail = jnp.concatenate([lists[...].astype(jnp.float32), jnp.zeros((4, LANES), jnp.float32)], axis=0)
    out[:, LIST_ROW:PIECE, :] = jnp.broadcast_to(tail[None], (HAD, 8, LANES))


def swap_segments(values):
    values = list(values)
    lane = lax.broadcasted_iota(jnp.int32, values[0].shape, values[0].ndim - 1)
    for bit in range(3):
        step = 1 << bit
        upper = jnp.bitwise_and(jnp.right_shift(lane, 4 + bit), 1) == 1
        for low in range(8):
            if low & step:
                continue
            first, second = values[low], values[low + step]
            values[low] = jnp.where(upper, pltpu.roll(second, 16 * step, 1), first)
            values[low + step] = jnp.where(upper, second, pltpu.roll(first, LANES - 16 * step, 1))
    return values


def signs(row_bits, count):
    both = jnp.bitwise_and(lax.broadcasted_iota(jnp.int32, (count, row_bits.shape[1]), 0), row_bits)
    for shift in (4, 2, 1):
        both = jnp.bitwise_xor(both, jnp.right_shift(both, shift))
    return (1 - 2 * jnp.bitwise_and(both, 1)).astype(jnp.float32)


def mix_kernel(pieces, sent, mixed, lists, table, picked, extra, out, arrived):
    scale = 1.0 / math.sqrt(ROWS * HAD)

    def butterfly(chunk, _):
        rows = pl.ds(pl.multiple_of(chunk * 8, 8), 8)
        values = [pieces[device, rows, :] for device in range(HAD)]
        for bit in range(5):
            step = 1 << bit
            for low in range(HAD):
                if low & step:
                    continue
                first, second = values[low], values[low + step]
                values[low], values[low + step] = first + second, first - second
        for source in range(HAD):
            mixed[source, rows, :] = values[source]
        return 0

    lax.fori_loop(0, LIST_ROW // 8, butterfly, 0)
    for high in range(4):
        received = [pieces[high * 8 + low, LIST_ROW:PIECE, :] for low in range(8)]
        for low, value in enumerate(swap_segments(received)):
            lists[low, :, high * LANES : (high + 1) * LANES] = value

    def sending(group):
        rows = pl.ds(pl.multiple_of(group * 32, 32), 32)
        return pltpu.make_async_copy(out.at[:, rows, :], sent.at[:, rows, :], arrived.at[group])

    def source_group(group, _):
        for low in range(8):
            source = group * 8 + low
            rows = lists[low, pl.ds(group, 1), :].astype(jnp.int32)
            fine = signs(jnp.bitwise_and(rows, 31), 32).astype(jnp.bfloat16)
            coarse = signs(jnp.right_shift(rows, 5), 32).astype(jnp.bfloat16)
            for step in range(32):
                table[low % 2, step * 32 : (step + 1) * 32, :] = fine * coarse[step : step + 1, :]
            main = jnp.concatenate([mixed[source, t * 32 : (t + 1) * 32, :] for t in range(8)], axis=1)
            tail = mixed[source, 256:272, :]
            tail = jnp.concatenate([tail[2 * t : 2 * t + 2, :] for t in range(8)], axis=1)
            main_high = main.astype(jnp.bfloat16).astype(jnp.float32)
            tail_high = tail.astype(jnp.bfloat16).astype(jnp.float32)
            left = jnp.concatenate(
                [
                    main_high,
                    main - main_high,
                    tail_high,
                    tail - tail_high,
                    jnp.zeros((4, ROWS), jnp.float32),
                ],
                axis=0,
            ).astype(jnp.bfloat16)
            product = jnp.dot(left, table[low % 2], preferred_element_type=jnp.float32)
            picked[low, 0:32, :] = (product[0:32] + product[32:64]) * scale
            picked[low, 32:34, :] = (product[64:66] + product[66:68]) * scale
        for high in range(4):
            lanes = slice(high * LANES, (high + 1) * LANES)
            moved = swap_segments([picked[low, :, lanes] for low in range(8)])
            for low, value in enumerate(moved):
                out[high * 8 + low, pl.ds(pl.multiple_of(group * 32, 32), 32), :] = value[0:32]
                extra[group, high * 8 + low] = value[32:40]
        sending(group).start()
        return 0

    lax.fori_loop(0, 4, source_group, 0)
    for group in range(4):
        for owner in range(HAD):
            out[owner, 128 + 2 * group : 130 + 2 * group, :] = extra[group, owner, 0:2, :]
    last = pltpu.make_async_copy(out.at[:, 128:BACK, :], sent.at[:, 128:BACK, :], arrived.at[4])
    last.start()
    for group in range(4):
        sending(group).wait()
    last.wait()


def gram_kernel(slot_total, received, counts, core, mine, other, sketch_out, flipped, gram, sketch, arrived):
    size = PACKED // 2
    sending = []
    lane = lax.broadcasted_iota(jnp.int32, (1, LANES), 1)
    segment, slot = jnp.right_shift(lane, 4), jnp.bitwise_and(lane, CAP - 1)
    for group in range(4):
        lanes = slice(group * LANES, (group + 1) * LANES)
        live = jnp.zeros((1, LANES), jnp.int32)
        for low in range(8):
            live = jnp.where(segment == low, counts[0, 8 * group + low], live)
        keep = slot < live
        part = received[:, group * 32 : (group + 1) * 32, :].reshape(D, LANES)
        part = jnp.where(keep, part, 0.0)
        flipped[0:D, lanes] = part * (1.0 / slot_total)
        sketch[lanes, :] = part.T
        sending.append(pltpu.make_async_copy(sketch.at[lanes, :], sketch_out.at[lanes, :], arrived.at[group]))
        sending[-1].start()
        for half in range(2):
            for device in range(HAD):
                row = D + 32 * half + device
                source = 128 + 2 * group + half
                value = received[device, source : source + 1, :]
                flipped[row : row + 1, lanes] = jnp.where(keep, value, 0.0) * (1.0 / slot_total)
    for pair in range(BLOCKS // 2):
        first = 256 * pair
        block = times_by_parts(flipped[first:, :], sketch[:, first : first + 256])
        left, right = 2 * pair, 2 * pair + 1
        gram[COLUMN_START[left] : COLUMN_START[left] + COLUMN_ROWS[left], :] = block[:, :BLOCK]
        gram[COLUMN_START[right] : COLUMN_START[right] + COLUMN_ROWS[right], :] = block[BLOCK:, BLOCK:]
    for place, target in enumerate((mine, other)):
        first = pl.multiple_of(jnp.bitwise_xor(core[0], place) * size, size)
        sending.append(pltpu.make_async_copy(gram.at[pl.ds(first, size), :], target, arrived.at[4 + place]))
        sending[-1].start()
    for copy in sending:
        copy.wait()


def across_lanes(value, lane):
    return jnp.broadcast_to(value[:, lane : lane + 1], value.shape)


def down_rows(value, row):
    return jnp.broadcast_to(value[row : row + 1, :], value.shape)


def inverse_factor(block, beyond):
    rows = [[block[8 * g : 8 * g + 8, :]] for g in range(16)]
    sub = lax.broadcasted_iota(jnp.int32, (8, LANES), 0)
    lane = lax.broadcasted_iota(jnp.int32, (8, LANES), 1)
    result, products = [], []
    for g in range(16):
        if g == LAST_RUN and beyond is not None:
            mixed = jnp.concatenate([rows[h][0] for h in range(g, 16)], axis=0)
            done = lax.broadcasted_iota(jnp.int32, mixed.shape, 1) < 8 * g
            carried = beyond[8 * g :, :] + times(jnp.where(done, mixed, 0.0), beyond)
            for h in range(g, 16):
                rows[h].append(carried[8 * (h - g) : 8 * (h - g) + 8, :])
        own = jnp.right_shift(lane, 3) == g
        columns = [across_lanes(rows[g][0], 8 * g + k) for k in range(8)]
        values = [jnp.where(own, jnp.where(lane == 8 * g + sub, 1.0, 0.0), rows[g][0])] + rows[g][1:]
        finished = [jnp.zeros((8, LANES), jnp.float32) for _ in values]
        for i in range(8):
            here = sub == i
            weight = columns[i]
            pivot = down_rows(weight, i)
            inverse = 1.0 / pivot
            root = lax.rsqrt(pivot)
            root = root * (1.5 - 0.5 * pivot * root * root)

            def eliminate(held, entry):
                return jnp.where(here, 0.0, held) - jnp.where(here, -entry, weight * entry) * inverse

            for n in range(len(values)):
                entry = down_rows(values[n], i)
                finished[n] = jnp.where(here, entry * root, finished[n])
                values[n] = eliminate(values[n], entry)
            for k in range(i + 1, 8):
                columns[k] = eliminate(columns[k], down_rows(columns[k], i))
        result.append(jnp.where(lane <= 8 * g + sub, finished[0], 0.0))
        products += finished[1:]
        solved = [[down_rows(value, k) for k in range(8)] for value in values]
        far = 16 if g >= LAST_RUN else min(16, g + 1 + NEAR_ROWS)
        for h in range(g + 1, far):
            spread = [across_lanes(rows[h][0], 8 * g + k) for k in range(8)]
            for n in range(len(values)):
                terms = [spread[k] * solved[n][k] for k in range(8)]
                while len(terms) > 1:
                    terms = [terms[t] + terms[t + 1] for t in range(0, len(terms), 2)]
                held = jnp.where(own, 0.0, rows[h][0]) if n == 0 else rows[h][n]
                rows[h][n] = held - terms[0]
        if far < 16:
            left = jnp.concatenate([jnp.where(own, rows[h][0], 0.0) for h in range(far, 16)], axis=0)
            right = [values[0], jnp.zeros((LANES - 8 * g - 8, LANES), jnp.float32)]
            if g > 0:
                right.insert(0, jnp.zeros((8 * g, LANES), jnp.float32))
            change = times(left, jnp.concatenate(right, axis=0))
            for h in range(far, 16):
                rows[h][0] = jnp.where(own, 0.0, rows[h][0]) - change[8 * (h - far) : 8 * (h - far) + 8, :]
        yield result, products


def times_transposed(left, right):
    return lax.dot_general(
        left,
        right,
        (((1,), (1,)), ((), ())),
        precision=HIGHEST,
        preferred_element_type=jnp.float32,
    )


def times(left, right):
    return jnp.dot(left, right, precision=HIGHEST, preferred_element_type=jnp.float32)


def halves(value):
    high = value.astype(jnp.bfloat16)
    return high, (value - high.astype(jnp.float32)).astype(jnp.bfloat16)


def times_by_parts(left, right):
    left_high, left_low = halves(left)
    right_high, right_low = halves(right)
    return jnp.dot(
        jnp.concatenate([left_high, left_high, left_low], axis=1),
        jnp.concatenate([right_high, right_low, right_high], axis=0),
        preferred_element_type=jnp.float32,
    )


def beside(steps, tasks, watch):
    tasks, left = list(tasks), 16
    while True:
        try:
            seen, products = next(steps)
        except StopIteration:
            return jnp.concatenate(seen, axis=0)
        for _ in range(-(-len(tasks) // left)):
            tasks.pop(0)()
        watch(seen, products)
        left = max(left - 1, 1)


def solve_kernel(part, other, sketch_in, core, basis_out, answer, lower, inverted, flipped, sketch, basis, arrived):
    size = PACKED // 2
    loading = []
    for place, source in enumerate((part, other)):
        first = pl.multiple_of(jnp.bitwise_xor(core[0], place) * size, size)
        loading.append(pltpu.make_async_copy(source, lower.at[pl.ds(first, size), :], arrived.at[place]))
    for copy in loading:
        copy.start()
    sketch_copy = pltpu.make_async_copy(sketch_in, sketch, arrived.at[2])
    sketch_copy.start()
    row = lax.broadcasted_iota(jnp.int32, (BLOCK, BLOCK), 0)
    column = lax.broadcasted_iota(jnp.int32, (BLOCK, BLOCK), 1)
    ridge = jnp.where(row == column, RIDGE, 0.0)

    def at(i, j, end=None):
        start = COLUMN_START[j] + BLOCK * (i - j)
        last = COLUMN_START[j] + (COLUMN_ROWS[j] if end == 9 else BLOCK * ((i if end is None else end) + 1 - j))
        return slice(start, last)

    def pieces_of(first, alone=True):
        pieces = [(first, first)] if alone and first < BLOCKS - 1 else []
        first += len(pieces)
        while first < BLOCKS:
            last = min(first + 1, BLOCKS - 1)
            pieces.append((first, 9 if last == BLOCKS - 1 else last))
            first = last + 1
        return pieces or [(BLOCKS, 9)]

    def saving(pair):
        columns = slice(2 * BLOCK * pair, 2 * BLOCK * (pair + 1))
        return pltpu.make_async_copy(basis.at[:, columns], basis_out.at[:, columns], arrived.at[3 + pair])

    def panel_tasks(k, upright):
        def rows_task(first, last):
            def task():
                rows = at(first, k, last)
                lower[rows, :] = times(lower[rows, :], upright)

            return task

        def sketch_task(part):
            def task():
                rows = slice(BLOCK * part, BLOCK * (part + 1))
                own = slice(BLOCK * k, BLOCK * (k + 1))
                source = sketch if k == 0 else basis
                basis[rows, own] = times_by_parts(source[rows, own], upright)

            return task

        return [rows_task(*piece) for piece in pieces_of(k + 2)], [sketch_task(part) for part in range(4)]

    def near_tasks(k, upright):
        def rows_task(first, last):
            def task():
                rows = at(first, k + 1, last)
                lower[rows, :] = lower[rows, :] - times(lower[at(first, k, last), :], upright)

            return task

        def corner_task():
            value = lower[at(k + 2, k), :]
            rows = at(k + 2, k + 2)
            lower[rows, :] = lower[rows, :] - times_transposed(value, value)

        def sketch_task(part):
            def task():
                rows = slice(BLOCK * part, BLOCK * (part + 1))
                own = slice(BLOCK * k, BLOCK * (k + 1))
                beyond = slice(BLOCK * (k + 1), BLOCK * (k + 2))
                source = sketch if k < 2 else basis
                basis[rows, beyond] = source[rows, beyond] - times_by_parts(basis[rows, own], upright)

            return task

        above = [rows_task(*piece) for piece in pieces_of(k + 2)]
        if k + 2 < BLOCKS:
            above.append(corner_task)
        return above, [sketch_task(part) for part in range(4)]

    def wide(first, last, k):
        return jnp.concatenate([lower[at(first, k - 1, last), :], lower[at(first, k, last), :]], axis=1)

    def far_tasks(k):
        above, below = [], []

        def flip_task(c):
            def task():
                flipped[:, BLOCK * c : BLOCK * (c + 2)] = wide(c, c + 1, k).T

            return task

        def rows_task(c, first, last):
            def task():
                change = times(wide(first, last, k), flipped[:, BLOCK * c : BLOCK * (c + 2)])
                if first == c:
                    if c > k + 1:
                        rows = at(c, c)
                        lower[rows, :] = lower[rows, :] - change[:BLOCK, :BLOCK]
                    rows = at(c + 1, c)
                    lower[rows, :] = lower[rows, :] - change[BLOCK : 2 * BLOCK, :BLOCK]
                    rows = at(c + 1, c + 1)
                    lower[rows, :] = lower[rows, :] - change[BLOCK : 2 * BLOCK, BLOCK:]
                    if last == 9:
                        for half in range(2):
                            rows = at(BLOCKS, c + half, 9)
                            lanes = slice(BLOCK * half, BLOCK * (half + 1))
                            lower[rows, :] = lower[rows, :] - change[2 * BLOCK :, lanes]
                else:
                    for half in range(2):
                        rows = at(first, c + half, last)
                        lanes = slice(BLOCK * half, BLOCK * (half + 1))
                        lower[rows, :] = lower[rows, :] - change[:, lanes]

            return task

        def sketch_task(c, part):
            def task():
                rows = slice(BLOCK * part, BLOCK * (part + 1))
                own = slice(BLOCK * (k - 1), BLOCK * (k + 1))
                beyond = slice(BLOCK * c, BLOCK * (c + 2))
                source = sketch if k < 2 else basis
                basis[rows, beyond] = source[rows, beyond] - times_by_parts(basis[rows, own], flipped[:, beyond])

            return task

        for c in range(k + 1, BLOCKS, 2):
            above.append(flip_task(c))
            above += [rows_task(c, *piece) for piece in pieces_of(c, False)]
            below += [sketch_task(c, part) for part in range(4)]
        return above, below

    def inverse_tasks(k, inverse):
        own = slice(BLOCK * k, BLOCK * (k + 1))

        def finish_task():
            if k > 0:
                inverted[own, : BLOCK * k] = -times_by_parts(inverse, inverted[own, : BLOCK * k])
            inverted[own, own] = inverse
            if k % 2 == 0:
                inverted[own, BLOCK * (k + 1) : BLOCK * (k + 2)] = jnp.zeros((BLOCK, BLOCK), jnp.float32)

        def answer_task():
            change = times_by_parts(lower[at(BLOCKS, k, 9), :], inverted[own, : BLOCK * (k + 1)])
            if k > 0:
                answer[:, : BLOCK * k] = answer[:, : BLOCK * k] + change[:, : BLOCK * k]
            answer[:, own] = change[:, BLOCK * k :]

        def next_task(first):
            def task():
                rows = slice(BLOCK * first, BLOCK * (k + 1))
                columns = slice(BLOCK * first, BLOCK * min(first + 2, k + 1))
                left = jnp.concatenate([lower[at(k + 1, j), :] for j in range(first, k + 1)], axis=1)
                inverted[BLOCK * (k + 1) : BLOCK * (k + 2), columns] = times_by_parts(left, inverted[rows, columns])

            return task

        return [finish_task, answer_task] + [next_task(first) for first in range(0, k + 1 if k + 1 < BLOCKS else 0, 2)]

    for copy in loading:
        copy.wait()
    for k in range(BLOCKS):
        block = lower[at(k, k), :] + ridge
        if k == 1:
            sketch_copy.wait()
        if k < BLOCKS - 1:
            beyond = lower[at(k + 1, k), :].T
        else:
            beyond = None

        def watch(seen, products):
            if k < BLOCKS - 1 and len(seen) in RUN_ENDS:
                part = times(jnp.concatenate(seen[RUN_ENDS[len(seen)] :], axis=0), beyond)
                next_upright.append(part)
                changes.append(times(part.T, part))
            if k < BLOCKS - 1 and len(seen) == 16:
                next_upright.append(jnp.concatenate(products, axis=0))
                change = changes[0]
                for more in changes[1:]:
                    change = change + more
                corner = at(k + 1, k + 1)
                lower[corner, :] = (lower[corner, :] - change) - times(next_upright[-1].T, next_upright[-1])

        changes, next_upright = [], []
        inverse = beside(inverse_factor(block, beyond), tasks if k else [], watch)
        if k > 0 and k % 2 == 0:
            saving(k // 2 - 1).start()
        upright = inverse.T
        if k < BLOCKS - 1:
            value_upright = jnp.concatenate(next_upright, axis=0)
            lower[at(k + 1, k), :] = value_upright.T
        above, below = panel_tasks(k, upright)
        if k == BLOCKS - 1:
            more_above, more_below = [], []
        elif k % 2 == 0:
            more_above, more_below = near_tasks(k, value_upright)
        else:
            more_above, more_below = far_tasks(k)
        extra = inverse_tasks(k, inverse)
        if k == BLOCKS - 1:
            tasks = above + extra + below
        else:
            early = above[:1] + (more_above[:1] if k % 2 == 0 else more_above[:2])
            for task in early:
                task()
            tasks = above[1:] + more_above[len(early) - 1 :] + below + extra + more_below
    for task in tasks:
        task()
    saving(BLOCKS // 2 - 1).start()
    for pair in range(BLOCKS // 2):
        saving(pair).wait()


def swap_cores(value):
    return lax.ppermute(value, "had", [(device, device ^ 1) for device in range(HAD)])


SOLVE_SCRATCH = [
    pltpu.VMEM((PACKED, LANES), jnp.float32),
    pltpu.VMEM((D, D), jnp.float32),
    pltpu.VMEM((2 * BLOCK, D), jnp.float32),
    pltpu.VMEM((SLOTS, D), jnp.float32),
    pltpu.VMEM((SLOTS, D), jnp.float32),
    pltpu.SemaphoreType.DMA((7,)),
]


def total(mine, other):
    part = mine + swap_cores(other)
    chips = [[2 * chip + own for chip in range(HAD // 2)] for own in range(2)]
    half = part.shape[0]
    part = part.reshape(HAD // 2, half // (HAD // 2), LANES)
    part = lax.all_to_all(part, "had", 0, 0, tiled=True, axis_index_groups=chips)
    part = jnp.sum(part, axis=0)
    size = lax.axis_size("grp")
    part = jnp.broadcast_to(part[None], (size, *part.shape))
    part = jnp.sum(lax.all_to_all(part, "grp", 0, 0, tiled=True), axis=0)
    part = jnp.broadcast_to(part[None], (HAD // 2, *part.shape))
    part = lax.all_to_all(part, "had", 0, 0, tiled=True, axis_index_groups=chips)
    part = part.reshape(half, LANES)
    return part, swap_cores(part)


def on_device(embeddings, targets, sign_bits, samples, counts):
    had_size = lax.axis_size("had")
    core = jnp.bitwise_and(lax.axis_index("had"), 1).astype(jnp.int32).reshape(1)
    (pieces,) = call(
        spread_kernel,
        [(pltpu.VMEM, f32(HAD, PIECE, LANES))],
        [
            pltpu.VMEM((ROWS, D), jnp.bfloat16),
            pltpu.VMEM((K, ROWS), jnp.bfloat16),
            pltpu.VMEM((8, LANES), jnp.int32),
            pltpu.SemaphoreType.DMA((6,)),
        ],
        12,
        (pltpu.HBM, embeddings),
        (pltpu.HBM, targets.T),
        (pltpu.HBM, sign_bits.reshape(8, LANES)),
        (pltpu.VMEM, samples.reshape(4, LANES)),
    )
    pieces = lax.all_to_all(pieces, "had", split_axis=0, concat_axis=0, tiled=True)
    (outgoing,) = call(
        mix_kernel,
        [(pltpu.HBM, f32(HAD, BACK, LANES))],
        [
            pltpu.VMEM((HAD, LIST_ROW, LANES), jnp.float32),
            pltpu.VMEM((8, 8, SLOTS), jnp.float32),
            pltpu.VMEM((2, ROWS, SLOTS), jnp.bfloat16),
            pltpu.VMEM((8, 40, SLOTS), jnp.float32),
            pltpu.VMEM((4, HAD, 8, LANES), jnp.float32),
            pltpu.VMEM((HAD, BACK, LANES), jnp.float32),
            pltpu.SemaphoreType.DMA((5,)),
        ],
        20,
        (pltpu.VMEM, pieces),
    )
    received = lax.all_to_all(outgoing, "had", split_axis=0, concat_axis=0, tiled=True)
    slot_total = lax.axis_size("grp") * had_size * SLOTS
    mine, other, sketch = call(
        lambda *refs: gram_kernel(slot_total, *refs),
        [
            (pltpu.HBM, f32(PACKED // 2, LANES)),
            (pltpu.HBM, f32(PACKED // 2, LANES)),
            (pltpu.HBM, f32(SLOTS, D)),
        ],
        [
            pltpu.VMEM((D + K, SLOTS), jnp.float32),
            pltpu.VMEM((PACKED, LANES), jnp.float32),
            pltpu.VMEM((SLOTS, D), jnp.float32),
            pltpu.SemaphoreType.DMA((6,)),
        ],
        16,
        (pltpu.VMEM, received),
        (pltpu.SMEM, counts),
        (pltpu.SMEM, core),
    )
    part, other = total(mine, other)
    basis, coefficients = call(
        solve_kernel,
        [(pltpu.HBM, f32(SLOTS, D)), (pltpu.VMEM, f32(K, D))],
        SOLVE_SCRATCH,
        24,
        (pl.ANY, part),
        (pl.ANY, other),
        (pltpu.HBM, sketch),
        (pltpu.SMEM, core),
    )
    return basis, coefficients.T


def solution(mesh):
    placed = (
        P(("grp", "had"), None),
        P(("grp", "had"), None),
        P(("grp", "had")),
        P(("grp", "had"), None, None),
        P(("grp", "had"), None),
    )
    return jax.shard_map(
        on_device,
        mesh=mesh,
        in_specs=placed,
        out_specs=(P(("grp", "had"), None), P()),
        check_vma=False,
    )
```

```python
import math

import jax
import jax.numpy as jnp
from jax import lax
from jax.experimental import pallas as pl
from jax.experimental.pallas import tpu as pltpu
from jax.sharding import PartitionSpec as P

D = 1024
K = 64
CAP = 16
HAD = 32
ROWS = 1024
SLOTS = 512
LANES = 128
BLOCK = 128
BLOCKS = D // BLOCK
RIDGE = 0.05
BOTH = ("grp", "had")

PIECE = 280
LIST_ROW = 272
BACK = 136
HIGHEST = lax.Precision.HIGHEST
COLUMN_ROWS = [D + K - BLOCK * j for j in range(BLOCKS)]
COLUMN_START = [sum(COLUMN_ROWS[:j]) for j in range(BLOCKS)]
PACKED = sum(COLUMN_ROWS)
MIB = 1024 * 1024
NEAR_ROWS = 2
RUN_ENDS = {8: 0, 14: 8}
LAST_RUN = 14


def call(kernel, outs, scratch, vmem_mib, *args):
    return pl.pallas_call(
        kernel,
        out_shape=[shape for _, shape in outs],
        in_specs=[pl.BlockSpec(memory_space=space) for space, _ in args],
        out_specs=[pl.BlockSpec(memory_space=space) for space, _ in outs],
        scratch_shapes=scratch,
        compiler_params=pltpu.CompilerParams(vmem_limit_bytes=vmem_mib * MIB),
    )(*[array for _, array in args])


def f32(*shape):
    return jax.ShapeDtypeStruct(shape, jnp.float32)


def spread_kernel(embeddings_in, targets_in, sign_bits_in, lists, out, embeddings, targets, sign_bits, arrived):
    small = [
        pltpu.make_async_copy(sign_bits_in, sign_bits, arrived.at[0]),
        pltpu.make_async_copy(targets_in, targets, arrived.at[1]),
    ]
    large = []
    for part in range(4):
        rows = slice(part * 256, (part + 1) * 256)
        large.append(pltpu.make_async_copy(embeddings_in.at[rows, :], embeddings.at[rows, :], arrived.at[2 + part]))
    for copy in small + large:
        copy.start()
    for copy in small:
        copy.wait()
    factor = (1 - 2 * sign_bits[...]).astype(jnp.float32)
    for tile in range(8):
        if tile % 2 == 0:
            large[tile // 2].wait()
        rows = slice(tile * LANES, (tile + 1) * LANES)
        sign = factor[tile : tile + 1, :]
        columns = embeddings[rows, :].astype(jnp.float32).T * sign
        out[:, tile * 32 : (tile + 1) * 32, :] = columns.reshape(HAD, 32, LANES)
        extra = targets[:, rows].astype(jnp.float32) * sign
        for device in range(HAD):
            for half in range(2):
                row = 256 + 2 * tile + half
                source = 32 * half + device
                out[device, row : row + 1, :] = extra[source : source + 1, :]
    by_source = lists[...].astype(jnp.float32).T
    numbers = [
        jnp.concatenate([by_source[8 * group + low : 8 * group + low + 1, :] for low in range(8)], axis=1)
        for group in range(4)
    ]
    tail = jnp.concatenate(numbers + [jnp.zeros((4, LANES), jnp.float32)], axis=0)
    out[:, LIST_ROW:PIECE, :] = jnp.broadcast_to(tail[None], (HAD, 8, LANES))


def swap_segments(values):
    values = list(values)
    lane = lax.broadcasted_iota(jnp.int32, values[0].shape, values[0].ndim - 1)
    for bit in range(3):
        step = 1 << bit
        upper = jnp.bitwise_and(jnp.right_shift(lane, 4 + bit), 1) == 1
        for low in range(8):
            if low & step:
                continue
            first, second = values[low], values[low + step]
            values[low] = jnp.where(upper, pltpu.roll(second, 16 * step, 1), first)
            values[low + step] = jnp.where(upper, second, pltpu.roll(first, LANES - 16 * step, 1))
    return values


def signs(row_bits, count):
    both = jnp.bitwise_and(lax.broadcasted_iota(jnp.int32, (count, row_bits.shape[1]), 0), row_bits)
    for shift in (4, 2, 1):
        both = jnp.bitwise_xor(both, jnp.right_shift(both, shift))
    return (1 - 2 * jnp.bitwise_and(both, 1)).astype(jnp.float32)


def split(value):
    high = value.astype(jnp.bfloat16).astype(jnp.float32)
    return high, value - high


def mix_kernel(pieces, sent, mixed, lists, table, picked, extra, out, arrived):
    scale = 1.0 / math.sqrt(ROWS * HAD)

    def butterfly(chunk, _):
        rows = pl.ds(pl.multiple_of(chunk * 8, 8), 8)
        values = [pieces[device, rows, :] for device in range(HAD)]
        for bit in range(5):
            step = 1 << bit
            for low in range(HAD):
                if low & step:
                    continue
                first, second = values[low], values[low + step]
                values[low], values[low + step] = first + second, first - second
        for source in range(HAD):
            mixed[source, rows, :] = values[source]
        return 0

    lax.fori_loop(0, LIST_ROW // 8, butterfly, 0)
    for high in range(4):
        received = [pieces[high * 8 + low, LIST_ROW:PIECE, :] for low in range(8)]
        for low, value in enumerate(swap_segments(received)):
            lists[low, :, high * LANES : (high + 1) * LANES] = value

    def sending(group):
        rows = pl.ds(pl.multiple_of(group * 32, 32), 32)
        return pltpu.make_async_copy(out.at[:, rows, :], sent.at[:, rows, :], arrived.at[group])

    def source_group(group, _):
        for low in range(8):
            source = group * 8 + low
            rows = lists[low, pl.ds(group, 1), :].astype(jnp.int32)
            fine = signs(jnp.bitwise_and(rows, 31), 32).astype(jnp.bfloat16)
            coarse = signs(jnp.bitwise_and(jnp.right_shift(rows, 5), 7), 8).astype(jnp.bfloat16)
            for step in range(8):
                table[low % 2, step * 32 : (step + 1) * 32, :] = fine * coarse[step : step + 1, :]
            tail = mixed[source, 256:272, :]
            mains, tails = [], []
            for quarter in range(4):
                tiles = (2 * quarter, 2 * quarter + 1)
                main = jnp.concatenate([mixed[source, t * 32 : (t + 1) * 32, :] for t in tiles], axis=1)
                mains += list(split(main))
                tails.append(jnp.concatenate([tail[2 * t : 2 * t + 2, :] for t in tiles], axis=1))
            left = jnp.concatenate(mains + list(split(jnp.concatenate(tails, axis=0))), axis=0).astype(jnp.bfloat16)
            product = jnp.dot(left, table[low % 2], preferred_element_type=jnp.float32)
            first = (1 - 2 * jnp.bitwise_and(jnp.right_shift(rows, 8), 1)).astype(jnp.float32)
            second = (1 - 2 * jnp.bitwise_and(jnp.right_shift(rows, 9), 1)).astype(jnp.float32) * scale
            main = [product[64 * n : 64 * n + 32] + product[64 * n + 32 : 64 * n + 64] for n in range(4)]
            picked[low, 0:32, :] = (main[0] + first * main[1]) * scale + second * (main[2] + first * main[3])
            ends = product[256:264] + product[264:272]
            ends = [ends[2 * n : 2 * n + 2] for n in range(4)]
            picked[low, 32:34, :] = (ends[0] + first * ends[1]) * scale + second * (ends[2] + first * ends[3])
        for high in range(4):
            lanes = slice(high * LANES, (high + 1) * LANES)
            moved = swap_segments([picked[low, :, lanes] for low in range(8)])
            for low, value in enumerate(moved):
                out[high * 8 + low, pl.ds(pl.multiple_of(group * 32, 32), 32), :] = value[0:32]
                extra[group, high * 8 + low] = value[32:40]
        sending(group).start()
        return 0

    lax.fori_loop(0, 4, source_group, 0)
    for group in range(4):
        for owner in range(HAD):
            out[owner, 128 + 2 * group : 130 + 2 * group, :] = extra[group, owner, 0:2, :]
    last = pltpu.make_async_copy(out.at[:, 128:BACK, :], sent.at[:, 128:BACK, :], arrived.at[4])
    last.start()
    for group in range(4):
        sending(group).wait()
    last.wait()


def gram_kernel(slot_total, received, counts, core, mine, other, sketch_out, flipped, gram, sketch, arrived):
    size = PACKED // 2
    sending = []
    lane = lax.broadcasted_iota(jnp.int32, (1, LANES), 1)
    segment, slot = jnp.right_shift(lane, 4), jnp.bitwise_and(lane, CAP - 1)
    for group in range(4):
        lanes = slice(group * LANES, (group + 1) * LANES)
        live = jnp.zeros((1, LANES), jnp.int32)
        for low in range(8):
            live = jnp.where(segment == low, counts[0, 8 * group + low], live)
        keep = slot < live
        part = received[:, group * 32 : (group + 1) * 32, :].reshape(D, LANES)
        part = jnp.where(keep, part, 0.0)
        flipped[0:D, lanes] = part * (1.0 / slot_total)
        sketch[lanes, :] = part.T
        sending.append(pltpu.make_async_copy(sketch.at[lanes, :], sketch_out.at[lanes, :], arrived.at[group]))
        sending[-1].start()
        for half in range(2):
            for device in range(HAD):
                row = D + 32 * half + device
                source = 128 + 2 * group + half
                value = received[device, source : source + 1, :]
                flipped[row : row + 1, lanes] = jnp.where(keep, value, 0.0) * (1.0 / slot_total)
    for pair in range(BLOCKS // 2):
        first = 256 * pair
        block = times_by_parts(flipped[first:, :], sketch[:, first : first + 256])
        left, right = 2 * pair, 2 * pair + 1
        gram[COLUMN_START[left] : COLUMN_START[left] + COLUMN_ROWS[left], :] = block[:, :BLOCK]
        gram[COLUMN_START[right] : COLUMN_START[right] + COLUMN_ROWS[right], :] = block[BLOCK:, BLOCK:]
    for place, target in enumerate((mine, other)):
        first = pl.multiple_of(jnp.bitwise_xor(core[0], place) * size, size)
        sending.append(pltpu.make_async_copy(gram.at[pl.ds(first, size), :], target, arrived.at[4 + place]))
        sending[-1].start()
    for copy in sending:
        copy.wait()


def across_lanes(value, lane):
    return jnp.broadcast_to(value[:, lane : lane + 1], value.shape)


def down_rows(value, row):
    return jnp.broadcast_to(value[row : row + 1, :], value.shape)


def inverse_factor(block, beyond):
    rows = [[block[8 * g : 8 * g + 8, :]] for g in range(16)]
    sub = lax.broadcasted_iota(jnp.int32, (8, LANES), 0)
    lane = lax.broadcasted_iota(jnp.int32, (8, LANES), 1)
    result, products = [], []
    for g in range(16):
        if g == LAST_RUN and beyond is not None:
            mixed = jnp.concatenate([rows[h][0] for h in range(g, 16)], axis=0)
            done = lax.broadcasted_iota(jnp.int32, mixed.shape, 1) < 8 * g
            carried = beyond[8 * g :, :] + times(jnp.where(done, mixed, 0.0), beyond)
            for h in range(g, 16):
                rows[h].append(carried[8 * (h - g) : 8 * (h - g) + 8, :])
        own = jnp.right_shift(lane, 3) == g
        columns = [across_lanes(rows[g][0], 8 * g + k) for k in range(8)]
        values = [jnp.where(own, jnp.where(lane == 8 * g + sub, 1.0, 0.0), rows[g][0])] + rows[g][1:]
        finished = [jnp.zeros((8, LANES), jnp.float32) for _ in values]
        for i in range(8):
            here = sub == i
            weight = columns[i]
            pivot = down_rows(weight, i)
            inverse = 1.0 / pivot
            root = lax.rsqrt(pivot)
            root = root * (1.5 - 0.5 * pivot * root * root)

            def eliminate(held, entry):
                return jnp.where(here, 0.0, held) - jnp.where(here, -entry, weight * entry) * inverse

            for n in range(len(values)):
                entry = down_rows(values[n], i)
                finished[n] = jnp.where(here, entry * root, finished[n])
                values[n] = eliminate(values[n], entry)
            for k in range(i + 1, 8):
                columns[k] = eliminate(columns[k], down_rows(columns[k], i))
        result.append(jnp.where(lane <= 8 * g + sub, finished[0], 0.0))
        products += finished[1:]
        solved = [[down_rows(value, k) for k in range(8)] for value in values]
        far = 16 if g >= LAST_RUN else min(16, g + 1 + NEAR_ROWS)
        for h in range(g + 1, far):
            spread = [across_lanes(rows[h][0], 8 * g + k) for k in range(8)]
            for n in range(len(values)):
                terms = [spread[k] * solved[n][k] for k in range(8)]
                while len(terms) > 1:
                    terms = [terms[t] + terms[t + 1] for t in range(0, len(terms), 2)]
                held = jnp.where(own, 0.0, rows[h][0]) if n == 0 else rows[h][n]
                rows[h][n] = held - terms[0]
        if far < 16:
            left = jnp.concatenate([jnp.where(own, rows[h][0], 0.0) for h in range(far, 16)], axis=0)
            right = [values[0], jnp.zeros((LANES - 8 * g - 8, LANES), jnp.float32)]
            if g > 0:
                right.insert(0, jnp.zeros((8 * g, LANES), jnp.float32))
            change = times(left, jnp.concatenate(right, axis=0))
            for h in range(far, 16):
                rows[h][0] = jnp.where(own, 0.0, rows[h][0]) - change[8 * (h - far) : 8 * (h - far) + 8, :]
        yield result, products


def times_transposed(left, right):
    return lax.dot_general(
        left,
        right,
        (((1,), (1,)), ((), ())),
        precision=HIGHEST,
        preferred_element_type=jnp.float32,
    )


def times(left, right):
    return jnp.dot(left, right, precision=HIGHEST, preferred_element_type=jnp.float32)


def halves(value):
    high = value.astype(jnp.bfloat16)
    return high, (value - high.astype(jnp.float32)).astype(jnp.bfloat16)


def times_by_parts(left, right):
    left_high, left_low = halves(left)
    right_high, right_low = halves(right)
    return jnp.dot(
        jnp.concatenate([left_high, left_high, left_low], axis=1),
        jnp.concatenate([right_high, right_low, right_high], axis=0),
        preferred_element_type=jnp.float32,
    )


def beside(steps, tasks, watch):
    tasks, left = list(tasks), 16
    while True:
        try:
            seen, products = next(steps)
        except StopIteration:
            return jnp.concatenate(seen, axis=0)
        for _ in range(-(-len(tasks) // left)):
            tasks.pop(0)()
        watch(seen, products)
        left = max(left - 1, 1)


def solve_kernel(part, other, sketch_in, core, basis_out, answer, lower, inverted, flipped, sketch, basis, arrived):
    size = PACKED // 2
    loading = []
    for place, source in enumerate((part, other)):
        first = pl.multiple_of(jnp.bitwise_xor(core[0], place) * size, size)
        loading.append(pltpu.make_async_copy(source, lower.at[pl.ds(first, size), :], arrived.at[place]))
    for copy in loading:
        copy.start()
    sketch_copy = pltpu.make_async_copy(sketch_in, sketch, arrived.at[2])
    sketch_copy.start()
    row = lax.broadcasted_iota(jnp.int32, (BLOCK, BLOCK), 0)
    column = lax.broadcasted_iota(jnp.int32, (BLOCK, BLOCK), 1)
    ridge = jnp.where(row == column, RIDGE, 0.0)

    def at(i, j, end=None):
        start = COLUMN_START[j] + BLOCK * (i - j)
        last = COLUMN_START[j] + (COLUMN_ROWS[j] if end == 9 else BLOCK * ((i if end is None else end) + 1 - j))
        return slice(start, last)

    def pieces_of(first, alone=True):
        pieces = [(first, first)] if alone and first < BLOCKS - 1 else []
        first += len(pieces)
        while first < BLOCKS:
            last = min(first + 1, BLOCKS - 1)
            pieces.append((first, 9 if last == BLOCKS - 1 else last))
            first = last + 1
        return pieces or [(BLOCKS, 9)]

    def saving(pair):
        columns = slice(2 * BLOCK * pair, 2 * BLOCK * (pair + 1))
        return pltpu.make_async_copy(basis.at[:, columns], basis_out.at[:, columns], arrived.at[3 + pair])

    def panel_tasks(k, upright):
        def rows_task(first, last):
            def task():
                rows = at(first, k, last)
                lower[rows, :] = times(lower[rows, :], upright)

            return task

        def sketch_task(part):
            def task():
                rows = slice(BLOCK * part, BLOCK * (part + 1))
                own = slice(BLOCK * k, BLOCK * (k + 1))
                source = sketch if k == 0 else basis
                basis[rows, own] = times_by_parts(source[rows, own], upright)

            return task

        return [rows_task(*piece) for piece in pieces_of(k + 2)], [sketch_task(part) for part in range(4)]

    def near_tasks(k, upright):
        def rows_task(first, last):
            def task():
                rows = at(first, k + 1, last)
                lower[rows, :] = lower[rows, :] - times(lower[at(first, k, last), :], upright)

            return task

        def corner_task():
            value = lower[at(k + 2, k), :]
            rows = at(k + 2, k + 2)
            lower[rows, :] = lower[rows, :] - times_transposed(value, value)

        def sketch_task(part):
            def task():
                rows = slice(BLOCK * part, BLOCK * (part + 1))
                own = slice(BLOCK * k, BLOCK * (k + 1))
                beyond = slice(BLOCK * (k + 1), BLOCK * (k + 2))
                source = sketch if k < 2 else basis
                basis[rows, beyond] = source[rows, beyond] - times_by_parts(basis[rows, own], upright)

            return task

        above = [rows_task(*piece) for piece in pieces_of(k + 2)]
        if k + 2 < BLOCKS:
            above.append(corner_task)
        return above, [sketch_task(part) for part in range(4)]

    def wide(first, last, k):
        return jnp.concatenate([lower[at(first, k - 1, last), :], lower[at(first, k, last), :]], axis=1)

    def far_tasks(k):
        above, below = [], []

        def flip_task(c):
            def task():
                flipped[:, BLOCK * c : BLOCK * (c + 2)] = wide(c, c + 1, k).T

            return task

        def rows_task(c, first, last):
            def task():
                change = times(wide(first, last, k), flipped[:, BLOCK * c : BLOCK * (c + 2)])
                if first == c:
                    if c > k + 1:
                        rows = at(c, c)
                        lower[rows, :] = lower[rows, :] - change[:BLOCK, :BLOCK]
                    rows = at(c + 1, c)
                    lower[rows, :] = lower[rows, :] - change[BLOCK : 2 * BLOCK, :BLOCK]
                    rows = at(c + 1, c + 1)
                    lower[rows, :] = lower[rows, :] - change[BLOCK : 2 * BLOCK, BLOCK:]
                    if last == 9:
                        for half in range(2):
                            rows = at(BLOCKS, c + half, 9)
                            lanes = slice(BLOCK * half, BLOCK * (half + 1))
                            lower[rows, :] = lower[rows, :] - change[2 * BLOCK :, lanes]
                else:
                    for half in range(2):
                        rows = at(first, c + half, last)
                        lanes = slice(BLOCK * half, BLOCK * (half + 1))
                        lower[rows, :] = lower[rows, :] - change[:, lanes]

            return task

        def sketch_task(c, part):
            def task():
                rows = slice(BLOCK * part, BLOCK * (part + 1))
                own = slice(BLOCK * (k - 1), BLOCK * (k + 1))
                beyond = slice(BLOCK * c, BLOCK * (c + 2))
                source = sketch if k < 2 else basis
                basis[rows, beyond] = source[rows, beyond] - times_by_parts(basis[rows, own], flipped[:, beyond])

            return task

        for c in range(k + 1, BLOCKS, 2):
            above.append(flip_task(c))
            above += [rows_task(c, *piece) for piece in pieces_of(c, False)]
            below += [sketch_task(c, part) for part in range(4)]
        return above, below

    def inverse_tasks(k, inverse):
        own = slice(BLOCK * k, BLOCK * (k + 1))

        def finish_task():
            if k > 0:
                inverted[own, : BLOCK * k] = -times_by_parts(inverse, inverted[own, : BLOCK * k])
            inverted[own, own] = inverse
            if k % 2 == 0:
                inverted[own, BLOCK * (k + 1) : BLOCK * (k + 2)] = jnp.zeros((BLOCK, BLOCK), jnp.float32)

        def answer_task():
            change = times_by_parts(lower[at(BLOCKS, k, 9), :], inverted[own, : BLOCK * (k + 1)])
            if k > 0:
                answer[:, : BLOCK * k] = answer[:, : BLOCK * k] + change[:, : BLOCK * k]
            answer[:, own] = change[:, BLOCK * k :]

        def next_task(first):
            def task():
                rows = slice(BLOCK * first, BLOCK * (k + 1))
                columns = slice(BLOCK * first, BLOCK * min(first + 2, k + 1))
                left = jnp.concatenate([lower[at(k + 1, j), :] for j in range(first, k + 1)], axis=1)
                inverted[BLOCK * (k + 1) : BLOCK * (k + 2), columns] = times_by_parts(left, inverted[rows, columns])

            return task

        return [finish_task, answer_task] + [next_task(first) for first in range(0, k + 1 if k + 1 < BLOCKS else 0, 2)]

    for copy in loading:
        copy.wait()
    for k in range(BLOCKS):
        block = lower[at(k, k), :] + ridge
        if k == 1:
            sketch_copy.wait()
        if k < BLOCKS - 1:
            beyond = lower[at(k + 1, k), :].T
        else:
            beyond = None

        def watch(seen, products):
            if k < BLOCKS - 1 and len(seen) in RUN_ENDS:
                part = times(jnp.concatenate(seen[RUN_ENDS[len(seen)] :], axis=0), beyond)
                next_upright.append(part)
                changes.append(times(part.T, part))
            if k < BLOCKS - 1 and len(seen) == 16:
                next_upright.append(jnp.concatenate(products, axis=0))
                change = changes[0]
                for more in changes[1:]:
                    change = change + more
                corner = at(k + 1, k + 1)
                lower[corner, :] = (lower[corner, :] - change) - times(next_upright[-1].T, next_upright[-1])

        changes, next_upright = [], []
        inverse = beside(inverse_factor(block, beyond), tasks if k else [], watch)
        if k > 0 and k % 2 == 0:
            saving(k // 2 - 1).start()
        upright = inverse.T
        if k < BLOCKS - 1:
            value_upright = jnp.concatenate(next_upright, axis=0)
            lower[at(k + 1, k), :] = value_upright.T
        above, below = panel_tasks(k, upright)
        if k == BLOCKS - 1:
            more_above, more_below = [], []
        elif k % 2 == 0:
            more_above, more_below = near_tasks(k, value_upright)
        else:
            more_above, more_below = far_tasks(k)
        extra = inverse_tasks(k, inverse)
        if k == BLOCKS - 1:
            tasks = above + extra + below
        else:
            early = above[:1] + (more_above[:1] if k % 2 == 0 else more_above[:2])
            for task in early:
                task()
            tasks = above[1:] + more_above[len(early) - 1 :] + below + extra + more_below
    for task in tasks:
        task()
    saving(BLOCKS // 2 - 1).start()
    for pair in range(BLOCKS // 2):
        saving(pair).wait()


def swap_cores(value):
    return lax.ppermute(value, "had", [(device, device ^ 1) for device in range(HAD)])


SOLVE_SCRATCH = [
    pltpu.VMEM((PACKED, LANES), jnp.float32),
    pltpu.VMEM((D, D), jnp.float32),
    pltpu.VMEM((2 * BLOCK, D), jnp.float32),
    pltpu.VMEM((SLOTS, D), jnp.float32),
    pltpu.VMEM((SLOTS, D), jnp.float32),
    pltpu.SemaphoreType.DMA((7,)),
]


def total(mine, other):
    part = mine + swap_cores(other)
    chips = [[2 * chip + own for chip in range(HAD // 2)] for own in range(2)]
    half = part.shape[0]
    part = part.reshape(HAD // 2, half // (HAD // 2), LANES)
    part = lax.all_to_all(part, "had", 0, 0, tiled=True, axis_index_groups=chips)
    part = jnp.sum(part, axis=0)
    size = lax.axis_size("grp")
    part = jnp.broadcast_to(part[None], (size, *part.shape))
    part = jnp.sum(lax.all_to_all(part, "grp", 0, 0, tiled=True), axis=0)
    part = jnp.broadcast_to(part[None], (HAD // 2, *part.shape))
    part = lax.all_to_all(part, "had", 0, 0, tiled=True, axis_index_groups=chips)
    part = part.reshape(half, LANES)
    return part, swap_cores(part)


def on_device(embeddings, targets, sign_bits, samples, counts):
    had_size = lax.axis_size("had")
    core = jnp.bitwise_and(lax.axis_index("had"), 1).astype(jnp.int32).reshape(1)
    (pieces,) = call(
        spread_kernel,
        [(pltpu.VMEM, f32(HAD, PIECE, LANES))],
        [
            pltpu.VMEM((ROWS, D), jnp.bfloat16),
            pltpu.VMEM((K, ROWS), jnp.bfloat16),
            pltpu.VMEM((8, LANES), jnp.int32),
            pltpu.SemaphoreType.DMA((6,)),
        ],
        12,
        (pltpu.HBM, embeddings),
        (pltpu.HBM, targets.T),
        (pltpu.HBM, sign_bits.reshape(8, LANES)),
        (pltpu.VMEM, samples.reshape(had_size, CAP).T),
    )
    pieces = lax.all_to_all(pieces, "had", split_axis=0, concat_axis=0, tiled=True)
    (outgoing,) = call(
        mix_kernel,
        [(pltpu.HBM, f32(HAD, BACK, LANES))],
        [
            pltpu.VMEM((HAD, LIST_ROW, LANES), jnp.float32),
            pltpu.VMEM((8, 8, SLOTS), jnp.float32),
            pltpu.VMEM((2, ROWS // 4, SLOTS), jnp.bfloat16),
            pltpu.VMEM((8, 40, SLOTS), jnp.float32),
            pltpu.VMEM((4, HAD, 8, LANES), jnp.float32),
            pltpu.VMEM((HAD, BACK, LANES), jnp.float32),
            pltpu.SemaphoreType.DMA((5,)),
        ],
        20,
        (pltpu.VMEM, pieces),
    )
    received = lax.all_to_all(outgoing, "had", split_axis=0, concat_axis=0, tiled=True)
    slot_total = lax.axis_size("grp") * had_size * SLOTS
    mine, other, sketch = call(
        lambda *refs: gram_kernel(slot_total, *refs),
        [
            (pltpu.HBM, f32(PACKED // 2, LANES)),
            (pltpu.HBM, f32(PACKED // 2, LANES)),
            (pltpu.HBM, f32(SLOTS, D)),
        ],
        [
            pltpu.VMEM((D + K, SLOTS), jnp.float32),
            pltpu.VMEM((PACKED, LANES), jnp.float32),
            pltpu.VMEM((SLOTS, D), jnp.float32),
            pltpu.SemaphoreType.DMA((6,)),
        ],
        16,
        (pltpu.VMEM, received),
        (pltpu.SMEM, counts),
        (pltpu.SMEM, core),
    )
    part, other = total(mine, other)
    basis, coefficients = call(
        solve_kernel,
        [(pltpu.HBM, f32(SLOTS, D)), (pltpu.VMEM, f32(K, D))],
        SOLVE_SCRATCH,
        24,
        (pl.ANY, part),
        (pl.ANY, other),
        (pltpu.HBM, sketch),
        (pltpu.SMEM, core),
    )
    return basis, coefficients.T


def solution(mesh):
    placed = (
        P(("grp", "had"), None),
        P(("grp", "had"), None),
        P(("grp", "had")),
        P(("grp", "had"), None, None),
        P(("grp", "had"), None),
    )
    return jax.shard_map(
        on_device,
        mesh=mesh,
        in_specs=placed,
        out_specs=(P(("grp", "had"), None), P()),
        check_vma=False,
    )
```

```python
import math

import jax
import jax.numpy as jnp
from jax import lax
from jax.experimental import pallas as pl
from jax.experimental.pallas import tpu as pltpu
from jax.sharding import PartitionSpec as P

D = 1024
K = 64
CAP = 16
HAD = 32
ROWS = 1024
SLOTS = 512
LANES = 128
BLOCK = 128
BLOCKS = D // BLOCK
RIDGE = 0.05
BOTH = ("grp", "had")

PIECE = 280
LIST_ROW = 272
BACK = 136
HIGHEST = lax.Precision.HIGHEST
COLUMN_ROWS = [D + K - BLOCK * j for j in range(BLOCKS)]
COLUMN_START = [sum(COLUMN_ROWS[:j]) for j in range(BLOCKS)]
PACKED = sum(COLUMN_ROWS)
MIB = 1024 * 1024
NEAR_ROWS = 2
RUN_ENDS = {8: 0, 14: 8}
LAST_RUN = 14


def call(kernel, outs, scratch, vmem_mib, *args):
    return pl.pallas_call(
        kernel,
        out_shape=[shape for _, shape in outs],
        in_specs=[pl.BlockSpec(memory_space=space) for space, _ in args],
        out_specs=[pl.BlockSpec(memory_space=space) for space, _ in outs],
        scratch_shapes=scratch,
        compiler_params=pltpu.CompilerParams(vmem_limit_bytes=vmem_mib * MIB),
    )(*[array for _, array in args])


def f32(*shape):
    return jax.ShapeDtypeStruct(shape, jnp.float32)


def spread_kernel(embeddings_in, targets_in, numbers_in, out, embeddings, targets, arrived):
    small = [pltpu.make_async_copy(targets_in, targets, arrived.at[0])]
    large = []
    for part in range(4):
        rows = slice(part * 256, (part + 1) * 256)
        large.append(pltpu.make_async_copy(embeddings_in.at[rows, :], embeddings.at[rows, :], arrived.at[1 + part]))
    for copy in small + large:
        copy.start()
    for copy in small:
        copy.wait()
    factor = (1 - 2 * numbers_in[0:8, :]).astype(jnp.float32)
    for tile in range(8):
        if tile % 2 == 0:
            large[tile // 2].wait()
        rows = slice(tile * LANES, (tile + 1) * LANES)
        sign = factor[tile : tile + 1, :]
        columns = embeddings[rows, :].astype(jnp.float32).T * sign
        out[:, tile * 32 : (tile + 1) * 32, :] = columns.reshape(HAD, 32, LANES)
        extra = targets[:, rows].astype(jnp.float32) * sign
        for device in range(HAD):
            for half in range(2):
                row = 256 + 2 * tile + half
                source = 32 * half + device
                out[device, row : row + 1, :] = extra[source : source + 1, :]
    by_source = numbers_in[8:24, :].astype(jnp.float32).T
    numbers = [
        jnp.concatenate([by_source[8 * group + low : 8 * group + low + 1, :] for low in range(8)], axis=1)
        for group in range(4)
    ]
    tail = jnp.concatenate(numbers + [jnp.zeros((4, LANES), jnp.float32)], axis=0)
    out[:, LIST_ROW:PIECE, :] = jnp.broadcast_to(tail[None], (HAD, 8, LANES))


def swap_segments(values):
    values = list(values)
    lane = lax.broadcasted_iota(jnp.int32, values[0].shape, values[0].ndim - 1)
    for bit in range(3):
        step = 1 << bit
        upper = jnp.bitwise_and(jnp.right_shift(lane, 4 + bit), 1) == 1
        for low in range(8):
            if low & step:
                continue
            first, second = values[low], values[low + step]
            values[low] = jnp.where(upper, pltpu.roll(second, 16 * step, 1), first)
            values[low + step] = jnp.where(upper, second, pltpu.roll(first, LANES - 16 * step, 1))
    return values


def signs(row_bits, count):
    both = jnp.bitwise_and(lax.broadcasted_iota(jnp.int32, (count, row_bits.shape[1]), 0), row_bits)
    for shift in (4, 2, 1):
        both = jnp.bitwise_xor(both, jnp.right_shift(both, shift))
    return (1 - 2 * jnp.bitwise_and(both, 1)).astype(jnp.float32)


def split(value):
    high = value.astype(jnp.bfloat16).astype(jnp.float32)
    return high, value - high


def mix_kernel(pieces, sent, mixed, lists, table, picked, extra, out, arrived):
    scale = 1.0 / math.sqrt(ROWS * HAD)

    def butterfly(chunk, _):
        rows = pl.ds(pl.multiple_of(chunk * 8, 8), 8)
        values = [pieces[device, rows, :] for device in range(HAD)]
        for bit in range(5):
            step = 1 << bit
            for low in range(HAD):
                if low & step:
                    continue
                first, second = values[low], values[low + step]
                values[low], values[low + step] = first + second, first - second
        for source in range(HAD):
            mixed[source, rows, :] = values[source]
        return 0

    lax.fori_loop(0, LIST_ROW // 8, butterfly, 0)
    for high in range(4):
        received = [pieces[high * 8 + low, LIST_ROW:PIECE, :] for low in range(8)]
        for low, value in enumerate(swap_segments(received)):
            lists[low, :, high * LANES : (high + 1) * LANES] = value

    def sending(group):
        rows = pl.ds(pl.multiple_of(group * 32, 32), 32)
        return pltpu.make_async_copy(out.at[:, rows, :], sent.at[:, rows, :], arrived.at[group])

    def source_group(group, _):
        for low in range(8):
            source = group * 8 + low
            rows = lists[low, pl.ds(group, 1), :].astype(jnp.int32)
            fine = signs(jnp.bitwise_and(rows, 31), 32).astype(jnp.bfloat16)
            coarse = signs(jnp.bitwise_and(jnp.right_shift(rows, 5), 7), 8).astype(jnp.bfloat16)
            for step in range(8):
                table[low % 2, step * 32 : (step + 1) * 32, :] = fine * coarse[step : step + 1, :]
            tail = mixed[source, 256:272, :]
            mains, tails = [], []
            for quarter in range(4):
                tiles = (2 * quarter, 2 * quarter + 1)
                main = jnp.concatenate([mixed[source, t * 32 : (t + 1) * 32, :] for t in tiles], axis=1)
                mains += list(split(main))
                tails.append(jnp.concatenate([tail[2 * t : 2 * t + 2, :] for t in tiles], axis=1))
            left = jnp.concatenate(mains + list(split(jnp.concatenate(tails, axis=0))), axis=0).astype(jnp.bfloat16)
            product = jnp.dot(left, table[low % 2], preferred_element_type=jnp.float32)
            first = (1 - 2 * jnp.bitwise_and(jnp.right_shift(rows, 8), 1)).astype(jnp.float32)
            second = (1 - 2 * jnp.bitwise_and(jnp.right_shift(rows, 9), 1)).astype(jnp.float32) * scale
            main = [product[64 * n : 64 * n + 32] + product[64 * n + 32 : 64 * n + 64] for n in range(4)]
            picked[low, 0:32, :] = (main[0] + first * main[1]) * scale + second * (main[2] + first * main[3])
            ends = product[256:264] + product[264:272]
            ends = [ends[2 * n : 2 * n + 2] for n in range(4)]
            picked[low, 32:34, :] = (ends[0] + first * ends[1]) * scale + second * (ends[2] + first * ends[3])
        for high in range(4):
            lanes = slice(high * LANES, (high + 1) * LANES)
            moved = swap_segments([picked[low, :, lanes] for low in range(8)])
            for low, value in enumerate(moved):
                out[high * 8 + low, pl.ds(pl.multiple_of(group * 32, 32), 32), :] = value[0:32]
                extra[group, high * 8 + low] = value[32:40]
        sending(group).start()
        return 0

    lax.fori_loop(0, 4, source_group, 0)
    for group in range(4):
        for owner in range(HAD):
            out[owner, 128 + 2 * group : 130 + 2 * group, :] = extra[group, owner, 0:2, :]
    last = pltpu.make_async_copy(out.at[:, 128:BACK, :], sent.at[:, 128:BACK, :], arrived.at[4])
    last.start()
    for group in range(4):
        sending(group).wait()
    last.wait()


def gram_kernel(slot_total, received, counts, core, mine, other, sketch_out, flipped, gram, sketch, arrived):
    size = PACKED // 2
    sending = []
    lane = lax.broadcasted_iota(jnp.int32, (1, LANES), 1)
    segment, slot = jnp.right_shift(lane, 4), jnp.bitwise_and(lane, CAP - 1)
    for group in range(4):
        lanes = slice(group * LANES, (group + 1) * LANES)
        live = jnp.zeros((1, LANES), jnp.int32)
        for low in range(8):
            live = jnp.where(segment == low, counts[0, 8 * group + low], live)
        keep = slot < live
        part = received[:, group * 32 : (group + 1) * 32, :].reshape(D, LANES)
        part = jnp.where(keep, part, 0.0)
        flipped[0:D, lanes] = part * (1.0 / slot_total)
        sketch[lanes, :] = part.T
        sending.append(pltpu.make_async_copy(sketch.at[lanes, :], sketch_out.at[lanes, :], arrived.at[group]))
        sending[-1].start()
        for half in range(2):
            for device in range(HAD):
                row = D + 32 * half + device
                source = 128 + 2 * group + half
                value = received[device, source : source + 1, :]
                flipped[row : row + 1, lanes] = jnp.where(keep, value, 0.0) * (1.0 / slot_total)
    for pair in range(BLOCKS // 2):
        first = 256 * pair
        block = times_by_parts(flipped[first:, :], sketch[:, first : first + 256])
        left, right = 2 * pair, 2 * pair + 1
        gram[COLUMN_START[left] : COLUMN_START[left] + COLUMN_ROWS[left], :] = block[:, :BLOCK]
        gram[COLUMN_START[right] : COLUMN_START[right] + COLUMN_ROWS[right], :] = block[BLOCK:, BLOCK:]
    for place, target in enumerate((mine, other)):
        first = pl.multiple_of(jnp.bitwise_xor(core[0], place) * size, size)
        sending.append(pltpu.make_async_copy(gram.at[pl.ds(first, size), :], target, arrived.at[4 + place]))
        sending[-1].start()
    for copy in sending:
        copy.wait()


def across_lanes(value, lane):
    return jnp.broadcast_to(value[:, lane : lane + 1], value.shape)


def down_rows(value, row):
    return jnp.broadcast_to(value[row : row + 1, :], value.shape)


def inverse_factor(block, beyond):
    rows = [[block[8 * g : 8 * g + 8, :]] for g in range(16)]
    sub = lax.broadcasted_iota(jnp.int32, (8, LANES), 0)
    lane = lax.broadcasted_iota(jnp.int32, (8, LANES), 1)
    result, products = [], []
    for g in range(16):
        if g == LAST_RUN and beyond is not None:
            mixed = jnp.concatenate([rows[h][0] for h in range(g, 16)], axis=0)
            done = lax.broadcasted_iota(jnp.int32, mixed.shape, 1) < 8 * g
            carried = beyond[8 * g :, :] + times(jnp.where(done, mixed, 0.0), beyond)
            for h in range(g, 16):
                rows[h].append(carried[8 * (h - g) : 8 * (h - g) + 8, :])
        own = jnp.right_shift(lane, 3) == g
        columns = [across_lanes(rows[g][0], 8 * g + k) for k in range(8)]
        values = [jnp.where(own, jnp.where(lane == 8 * g + sub, 1.0, 0.0), rows[g][0])] + rows[g][1:]
        finished = [jnp.zeros((8, LANES), jnp.float32) for _ in values]
        for i in range(8):
            here = sub == i
            weight = columns[i]
            pivot = down_rows(weight, i)
            inverse = 1.0 / pivot
            root = lax.rsqrt(pivot)
            root = root * (1.5 - 0.5 * pivot * root * root)

            def eliminate(held, entry):
                return jnp.where(here, 0.0, held) - jnp.where(here, -entry, weight * entry) * inverse

            for n in range(len(values)):
                entry = down_rows(values[n], i)
                finished[n] = jnp.where(here, entry * root, finished[n])
                values[n] = eliminate(values[n], entry)
            for k in range(i + 1, 8):
                columns[k] = eliminate(columns[k], down_rows(columns[k], i))
        result.append(jnp.where(lane <= 8 * g + sub, finished[0], 0.0))
        products += finished[1:]
        solved = [[down_rows(value, k) for k in range(8)] for value in values]
        far = 16 if g >= LAST_RUN else min(16, g + 1 + NEAR_ROWS)
        for h in range(g + 1, far):
            spread = [across_lanes(rows[h][0], 8 * g + k) for k in range(8)]
            for n in range(len(values)):
                terms = [spread[k] * solved[n][k] for k in range(8)]
                while len(terms) > 1:
                    terms = [terms[t] + terms[t + 1] for t in range(0, len(terms), 2)]
                held = jnp.where(own, 0.0, rows[h][0]) if n == 0 else rows[h][n]
                rows[h][n] = held - terms[0]
        if far < 16:
            left = jnp.concatenate([jnp.where(own, rows[h][0], 0.0) for h in range(far, 16)], axis=0)
            right = [values[0], jnp.zeros((LANES - 8 * g - 8, LANES), jnp.float32)]
            if g > 0:
                right.insert(0, jnp.zeros((8 * g, LANES), jnp.float32))
            change = times(left, jnp.concatenate(right, axis=0))
            for h in range(far, 16):
                rows[h][0] = jnp.where(own, 0.0, rows[h][0]) - change[8 * (h - far) : 8 * (h - far) + 8, :]
        yield result, products


def times_transposed(left, right):
    return lax.dot_general(
        left,
        right,
        (((1,), (1,)), ((), ())),
        precision=HIGHEST,
        preferred_element_type=jnp.float32,
    )


def times(left, right):
    return jnp.dot(left, right, precision=HIGHEST, preferred_element_type=jnp.float32)


def halves(value):
    high = value.astype(jnp.bfloat16)
    return high, (value - high.astype(jnp.float32)).astype(jnp.bfloat16)


def times_by_parts(left, right):
    left_high, left_low = halves(left)
    right_high, right_low = halves(right)
    return jnp.dot(
        jnp.concatenate([left_high, left_high, left_low], axis=1),
        jnp.concatenate([right_high, right_low, right_high], axis=0),
        preferred_element_type=jnp.float32,
    )


def beside(steps, tasks, watch):
    tasks, left = list(tasks), 16
    while True:
        try:
            seen, products = next(steps)
        except StopIteration:
            return jnp.concatenate(seen, axis=0)
        for _ in range(-(-len(tasks) // left)):
            tasks.pop(0)()
        watch(seen, products)
        left = max(left - 1, 1)


def solve_kernel(part, other, sketch_in, core, basis_out, answer, lower, inverted, flipped, sketch, basis, arrived):
    size = PACKED // 2
    loading = []
    for place, source in enumerate((part, other)):
        first = pl.multiple_of(jnp.bitwise_xor(core[0], place) * size, size)
        loading.append(pltpu.make_async_copy(source, lower.at[pl.ds(first, size), :], arrived.at[place]))
    for copy in loading:
        copy.start()
    sketch_copy = pltpu.make_async_copy(sketch_in, sketch, arrived.at[2])
    sketch_copy.start()
    row = lax.broadcasted_iota(jnp.int32, (BLOCK, BLOCK), 0)
    column = lax.broadcasted_iota(jnp.int32, (BLOCK, BLOCK), 1)
    ridge = jnp.where(row == column, RIDGE, 0.0)

    def at(i, j, end=None):
        start = COLUMN_START[j] + BLOCK * (i - j)
        last = COLUMN_START[j] + (COLUMN_ROWS[j] if end == 9 else BLOCK * ((i if end is None else end) + 1 - j))
        return slice(start, last)

    def pieces_of(first, alone=True):
        pieces = [(first, first)] if alone and first < BLOCKS - 1 else []
        first += len(pieces)
        while first < BLOCKS:
            last = min(first + 1, BLOCKS - 1)
            pieces.append((first, 9 if last == BLOCKS - 1 else last))
            first = last + 1
        return pieces or [(BLOCKS, 9)]

    def saving(pair):
        columns = slice(2 * BLOCK * pair, 2 * BLOCK * (pair + 1))
        return pltpu.make_async_copy(basis.at[:, columns], basis_out.at[:, columns], arrived.at[3 + pair])

    def panel_tasks(k, upright):
        def rows_task(first, last):
            def task():
                rows = at(first, k, last)
                lower[rows, :] = times(lower[rows, :], upright)

            return task

        def sketch_task(part):
            def task():
                rows = slice(BLOCK * part, BLOCK * (part + 1))
                own = slice(BLOCK * k, BLOCK * (k + 1))
                source = sketch if k == 0 else basis
                basis[rows, own] = times_by_parts(source[rows, own], upright)

            return task

        return [rows_task(*piece) for piece in pieces_of(k + 2)], [sketch_task(part) for part in range(4)]

    def near_tasks(k, upright):
        def rows_task(first, last):
            def task():
                rows = at(first, k + 1, last)
                lower[rows, :] = lower[rows, :] - times(lower[at(first, k, last), :], upright)

            return task

        def corner_task():
            value = lower[at(k + 2, k), :]
            rows = at(k + 2, k + 2)
            lower[rows, :] = lower[rows, :] - times_transposed(value, value)

        def sketch_task(part):
            def task():
                rows = slice(BLOCK * part, BLOCK * (part + 1))
                own = slice(BLOCK * k, BLOCK * (k + 1))
                beyond = slice(BLOCK * (k + 1), BLOCK * (k + 2))
                source = sketch if k < 2 else basis
                basis[rows, beyond] = source[rows, beyond] - times_by_parts(basis[rows, own], upright)

            return task

        above = [rows_task(*piece) for piece in pieces_of(k + 2)]
        if k + 2 < BLOCKS:
            above.append(corner_task)
        return above, [sketch_task(part) for part in range(4)]

    def wide(first, last, k):
        return jnp.concatenate([lower[at(first, k - 1, last), :], lower[at(first, k, last), :]], axis=1)

    def far_tasks(k):
        above, below = [], []

        def flip_task(c):
            def task():
                flipped[:, BLOCK * c : BLOCK * (c + 2)] = wide(c, c + 1, k).T

            return task

        def rows_task(c, first, last):
            def task():
                change = times(wide(first, last, k), flipped[:, BLOCK * c : BLOCK * (c + 2)])
                if first == c:
                    if c > k + 1:
                        rows = at(c, c)
                        lower[rows, :] = lower[rows, :] - change[:BLOCK, :BLOCK]
                    rows = at(c + 1, c)
                    lower[rows, :] = lower[rows, :] - change[BLOCK : 2 * BLOCK, :BLOCK]
                    rows = at(c + 1, c + 1)
                    lower[rows, :] = lower[rows, :] - change[BLOCK : 2 * BLOCK, BLOCK:]
                    if last == 9:
                        for half in range(2):
                            rows = at(BLOCKS, c + half, 9)
                            lanes = slice(BLOCK * half, BLOCK * (half + 1))
                            lower[rows, :] = lower[rows, :] - change[2 * BLOCK :, lanes]
                else:
                    for half in range(2):
                        rows = at(first, c + half, last)
                        lanes = slice(BLOCK * half, BLOCK * (half + 1))
                        lower[rows, :] = lower[rows, :] - change[:, lanes]

            return task

        def sketch_task(c, part):
            def task():
                rows = slice(BLOCK * part, BLOCK * (part + 1))
                own = slice(BLOCK * (k - 1), BLOCK * (k + 1))
                beyond = slice(BLOCK * c, BLOCK * (c + 2))
                source = sketch if k < 2 else basis
                basis[rows, beyond] = source[rows, beyond] - times_by_parts(basis[rows, own], flipped[:, beyond])

            return task

        for c in range(k + 1, BLOCKS, 2):
            above.append(flip_task(c))
            above += [rows_task(c, *piece) for piece in pieces_of(c, False)]
            below += [sketch_task(c, part) for part in range(4)]
        return above, below

    def inverse_tasks(k, inverse):
        own = slice(BLOCK * k, BLOCK * (k + 1))

        def finish_task():
            if k > 0:
                inverted[own, : BLOCK * k] = -times_by_parts(inverse, inverted[own, : BLOCK * k])
            inverted[own, own] = inverse
            if k % 2 == 0:
                inverted[own, BLOCK * (k + 1) : BLOCK * (k + 2)] = jnp.zeros((BLOCK, BLOCK), jnp.float32)

        def answer_task():
            change = times_by_parts(lower[at(BLOCKS, k, 9), :], inverted[own, : BLOCK * (k + 1)])
            if k > 0:
                answer[:, : BLOCK * k] = answer[:, : BLOCK * k] + change[:, : BLOCK * k]
            answer[:, own] = change[:, BLOCK * k :]

        def next_task(first):
            def task():
                rows = slice(BLOCK * first, BLOCK * (k + 1))
                columns = slice(BLOCK * first, BLOCK * min(first + 2, k + 1))
                left = jnp.concatenate([lower[at(k + 1, j), :] for j in range(first, k + 1)], axis=1)
                inverted[BLOCK * (k + 1) : BLOCK * (k + 2), columns] = times_by_parts(left, inverted[rows, columns])

            return task

        return [finish_task, answer_task] + [next_task(first) for first in range(0, k + 1 if k + 1 < BLOCKS else 0, 2)]

    for copy in loading:
        copy.wait()
    for k in range(BLOCKS):
        block = lower[at(k, k), :] + ridge
        if k == 1:
            sketch_copy.wait()
        if k < BLOCKS - 1:
            beyond = lower[at(k + 1, k), :].T
        else:
            beyond = None

        def watch(seen, products):
            if k < BLOCKS - 1 and len(seen) in RUN_ENDS:
                part = times(jnp.concatenate(seen[RUN_ENDS[len(seen)] :], axis=0), beyond)
                next_upright.append(part)
                changes.append(times(part.T, part))
            if k < BLOCKS - 1 and len(seen) == 16:
                next_upright.append(jnp.concatenate(products, axis=0))
                change = changes[0]
                for more in changes[1:]:
                    change = change + more
                corner = at(k + 1, k + 1)
                lower[corner, :] = (lower[corner, :] - change) - times(next_upright[-1].T, next_upright[-1])

        changes, next_upright = [], []
        inverse = beside(inverse_factor(block, beyond), tasks if k else [], watch)
        if k > 0 and k % 2 == 0:
            saving(k // 2 - 1).start()
        upright = inverse.T
        if k < BLOCKS - 1:
            value_upright = jnp.concatenate(next_upright, axis=0)
            lower[at(k + 1, k), :] = value_upright.T
        above, below = panel_tasks(k, upright)
        if k == BLOCKS - 1:
            more_above, more_below = [], []
        elif k % 2 == 0:
            more_above, more_below = near_tasks(k, value_upright)
        else:
            more_above, more_below = far_tasks(k)
        extra = inverse_tasks(k, inverse)
        if k == BLOCKS - 1:
            tasks = above + extra + below
        else:
            early = above[:1] + (more_above[:1] if k % 2 == 0 else more_above[:2])
            for task in early:
                task()
            tasks = above[1:] + more_above[len(early) - 1 :] + below + extra + more_below
    for task in tasks:
        task()
    saving(BLOCKS // 2 - 1).start()
    for pair in range(BLOCKS // 2):
        saving(pair).wait()


def swap_cores(value):
    return lax.ppermute(value, "had", [(device, device ^ 1) for device in range(HAD)])


SOLVE_SCRATCH = [
    pltpu.VMEM((PACKED, LANES), jnp.float32),
    pltpu.VMEM((D, D), jnp.float32),
    pltpu.VMEM((2 * BLOCK, D), jnp.float32),
    pltpu.VMEM((SLOTS, D), jnp.float32),
    pltpu.VMEM((SLOTS, D), jnp.float32),
    pltpu.SemaphoreType.DMA((7,)),
]


def total(mine, other):
    part = mine + swap_cores(other)
    chips = [[2 * chip + own for chip in range(HAD // 2)] for own in range(2)]
    half = part.shape[0]
    part = part.reshape(HAD // 2, half // (HAD // 2), LANES)
    part = lax.all_to_all(part, "had", 0, 0, tiled=True, axis_index_groups=chips)
    part = jnp.sum(part, axis=0)
    size = lax.axis_size("grp")
    part = jnp.broadcast_to(part[None], (size, *part.shape))
    part = jnp.sum(lax.all_to_all(part, "grp", 0, 0, tiled=True), axis=0)
    part = jnp.broadcast_to(part[None], (HAD // 2, *part.shape))
    part = lax.all_to_all(part, "had", 0, 0, tiled=True, axis_index_groups=chips)
    part = part.reshape(half, LANES)
    return part, swap_cores(part)


def on_device(embeddings, targets, sign_bits, samples, counts):
    had_size = lax.axis_size("had")
    core = jnp.bitwise_and(lax.axis_index("had"), 1).astype(jnp.int32).reshape(1)
    lists = jnp.pad(samples.reshape(had_size, CAP).T, ((0, 0), (0, LANES - had_size)))
    numbers = jnp.concatenate([sign_bits.reshape(8, LANES), lists], axis=0)
    (pieces,) = call(
        spread_kernel,
        [(pltpu.VMEM, f32(HAD, PIECE, LANES))],
        [
            pltpu.VMEM((ROWS, D), jnp.bfloat16),
            pltpu.VMEM((K, ROWS), jnp.bfloat16),
            pltpu.SemaphoreType.DMA((5,)),
        ],
        12,
        (pltpu.HBM, embeddings),
        (pltpu.HBM, targets.T),
        (pltpu.VMEM, numbers),
    )
    pieces = lax.all_to_all(pieces, "had", split_axis=0, concat_axis=0, tiled=True)
    (outgoing,) = call(
        mix_kernel,
        [(pltpu.HBM, f32(HAD, BACK, LANES))],
        [
            pltpu.VMEM((HAD, LIST_ROW, LANES), jnp.float32),
            pltpu.VMEM((8, 8, SLOTS), jnp.float32),
            pltpu.VMEM((2, ROWS // 4, SLOTS), jnp.bfloat16),
            pltpu.VMEM((8, 40, SLOTS), jnp.float32),
            pltpu.VMEM((4, HAD, 8, LANES), jnp.float32),
            pltpu.VMEM((HAD, BACK, LANES), jnp.float32),
            pltpu.SemaphoreType.DMA((5,)),
        ],
        20,
        (pltpu.VMEM, pieces),
    )
    received = lax.all_to_all(outgoing, "had", split_axis=0, concat_axis=0, tiled=True)
    slot_total = lax.axis_size("grp") * had_size * SLOTS
    mine, other, sketch = call(
        lambda *refs: gram_kernel(slot_total, *refs),
        [
            (pltpu.HBM, f32(PACKED // 2, LANES)),
            (pltpu.HBM, f32(PACKED // 2, LANES)),
            (pltpu.HBM, f32(SLOTS, D)),
        ],
        [
            pltpu.VMEM((D + K, SLOTS), jnp.float32),
            pltpu.VMEM((PACKED, LANES), jnp.float32),
            pltpu.VMEM((SLOTS, D), jnp.float32),
            pltpu.SemaphoreType.DMA((6,)),
        ],
        16,
        (pltpu.VMEM, received),
        (pltpu.SMEM, counts),
        (pltpu.SMEM, core),
    )
    part, other = total(mine, other)
    basis, coefficients = call(
        solve_kernel,
        [(pltpu.HBM, f32(SLOTS, D)), (pltpu.VMEM, f32(K, D))],
        SOLVE_SCRATCH,
        24,
        (pl.ANY, part),
        (pl.ANY, other),
        (pltpu.HBM, sketch),
        (pltpu.SMEM, core),
    )
    return basis, coefficients.T


def solution(mesh):
    placed = (
        P(("grp", "had"), None),
        P(("grp", "had"), None),
        P(("grp", "had")),
        P(("grp", "had"), None, None),
        P(("grp", "had"), None),
    )
    return jax.shard_map(
        on_device,
        mesh=mesh,
        in_specs=placed,
        out_specs=(P(("grp", "had"), None), P()),
        check_vma=False,
    )
```
